32 devices in a mesh: clip: 8 (over y, x, core), feat: 4 (over z).
Axes of the slice: x: 2, y: 2, z: 4, core: 2. Of those that a mesh axis runs over, the one named last changes fastest.
Arguments:
- features: float32 [6144, 22528], P('clip', 'feat'), may hold values from -20 to 20
- weights: float32 [400, 22528], P(None, 'feat'), may hold values from -0.02665009 to 0.02665009
- labels: int32 [6144], P('clip'), may hold values from 0 to 399
Outputs:
- new_weights: float32 [400, 22528], P(None, 'feat')
- residual: float32 [400, 22528], P(None, 'feat')
The draws below stay inside these ranges and needn't reach their ends.
All inputs are finite; a program needn't handle non-finite values.
Results may differ from the reference program's by a relative error of at most 0.0003.
Values sent between devices are 32-bit elements; how exact they have to be, the bound alone decides.
No kernel may reach another device: no remote copies, remote signals or barrier semaphores. Data moves between devices by JAX's collectives and lax.ppermute only.
A program may use at most 128 MiB of HBM per device.

```python
import math
import jax
import jax.numpy as jnp
from jax import lax

FEATS = 22528
CLASSES = 400
ITERS = 2
ROWS = 6144


def shared_weights(key):
    noise = jax.random.normal(jax.random.fold_in(key, 11), (CLASSES, FEATS), jnp.float32)
    return jnp.clip(noise, -4.0, 4.0) / math.sqrt(FEATS)


def draw_weights(key, part):
    return shared_weights(key)


def draw_features(key, part):
    keyset = jax.random.split(jax.random.fold_in(key, 23), 1)
    noise = jnp.clip(jax.random.normal(keyset[0], (ROWS, FEATS), jnp.float32), -5.0, 5.0)
    return jnp.clip(noise, -20.0, 20.0)


def place_ends(values, key, smallest, high):
    shape = values.shape
    spot = [jax.random.randint(jax.random.fold_in(key, axis), (), 0, shape[axis]) for axis in range(len(shape))]
    values = values.at[tuple(spot)].set(smallest)
    longest = shape.index(max(shape))
    spot[longest] = (spot[longest] + 1) % shape[longest]
    return values.at[tuple(spot)].set(high)


def setup_inputs(seed: int = 0) -> dict:
    key_list = jax.random.split(jax.random.key(seed), 4)
    return {
        "features": draw_features(jax.random.fold_in(key_list[3], 71), 0),
        "weights": draw_weights(jax.random.fold_in(key_list[3], 71), 0),
        "labels": place_ends(jax.random.randint(key_list[2], (ROWS,), 0, CLASSES), jax.random.fold_in(key_list[2], 1), 0, CLASSES - 1).astype(jnp.int32),
    }


damping = 0.01


def reference(features, weights, labels):
    highest = lax.Precision.HIGHEST
    logits = jnp.dot(features, weights.T, precision=highest, preferred_element_type=jnp.float32)
    probs = jax.nn.softmax(logits, axis=1)
    onehot = (labels[:, None] == jnp.arange(CLASSES, dtype=jnp.int32)[None, :]).astype(jnp.float32)
    gradient = jnp.dot((probs - onehot).T, features, precision=highest, preferred_element_type=jnp.float32) / ROWS

    def operate(vector):
        tangent = jnp.dot(features, vector.T, precision=highest, preferred_element_type=jnp.float32)
        bent = probs * tangent - probs * jnp.sum(probs * tangent, axis=1, keepdims=True)
        back = jnp.dot(bent.T, features, precision=highest, preferred_element_type=jnp.float32)
        return back / ROWS + damping * vector

    solution = jnp.zeros_like(weights)
    residual = -gradient
    direction = residual
    norm_now = jnp.sum(residual * residual)
    for iteration in range(ITERS):
        image = operate(direction)
        step_size = norm_now / jnp.sum(direction * image)
        solution = solution + step_size * direction
        residual = residual - step_size * image
        norm_next = jnp.sum(residual * residual)
        direction = residual + (norm_next / norm_now) * direction
        norm_now = norm_next
    return weights + solution, residual
```

```python
import jax
import jax.numpy as jnp
from jax import lax
from jax.sharding import PartitionSpec as P

damping = 0.01
HIGH = lax.Precision.HIGH


def chunks_of(classes, parts):
    eighths = classes // 8
    starts = [8 * (eighths * k // parts) for k in range(parts)] + [classes]
    return list(zip(starts[:-1], starts[1:]))


def back(row_values, features):
    return lax.dot_general(
        row_values, features, (((1,), (0,)), ((), ())), precision=HIGH, preferred_element_type=jnp.float32
    )


def forth(vectors, features):
    return lax.dot_general(
        vectors, features, (((1,), (1,)), ((), ())), precision=HIGH, preferred_element_type=jnp.float32
    )


def local(features, weights, labels):
    rows = features.shape[0]
    classes = weights.shape[0]
    n_clip, n_feat = lax.axis_size("clip"), lax.axis_size("feat")
    total_rows = rows * n_clip
    ranges = chunks_of(classes, 2)

    def sum_feat(x):
        return lax.psum(x, "feat")

    def sum_clip(x):
        return lax.psum(x, "clip")

    def backward(row_values):
        return [sum_clip(back(row_values[a:b], features)) for a, b in ranges]

    def forward(vectors):
        return [sum_feat(forth(v, features)) for v in vectors]

    def bend(probs, tangent):
        weighted = probs * tangent
        return (weighted - probs * jnp.sum(weighted, axis=0, keepdims=True)) / total_rows

    logits = sum_feat(forth(weights, features))
    top = jnp.max(logits, axis=0, keepdims=True)
    powers = jnp.exp(logits - top)
    probs = powers / jnp.sum(powers, axis=0, keepdims=True)
    onehot = (labels[None, :] == jnp.arange(classes, dtype=jnp.int32)[:, None]).astype(jnp.float32)

    direction = [-g for g in backward((probs - onehot) / total_rows)]
    tangent = jnp.concatenate(forward(direction), axis=0)
    bent = bend(probs, tangent)
    norm = sum(jnp.sum(d * d) for d in direction)
    both = lax.psum(jnp.stack([norm / n_clip, jnp.sum(bent * tangent) / n_feat]), ("clip", "feat"))
    norm0, curvature0 = both[0], both[1] + damping * both[0]
    step0 = norm0 / curvature0

    image = backward(bent)
    residual = [d - step0 * (i + damping * d) for d, i in zip(direction, image)]
    inner = jnp.stack([
        sum(jnp.sum(r * r) for r in residual),
        sum(jnp.sum(r * d) for r, d in zip(residual, direction)),
    ])
    inner = lax.psum(inner, "feat")
    norm1 = inner[0]
    ratio = norm1 / norm0
    tangent = jnp.concatenate(forward(residual), axis=0) + ratio * tangent
    bent = bend(probs, tangent)
    length = norm1 + 2.0 * ratio * inner[1] + ratio * ratio * norm0
    curvature1 = lax.psum(jnp.sum(bent * tangent), "clip") + damping * length
    step1 = norm1 / curvature1

    image = backward(bent)
    following = [r + ratio * d for r, d in zip(residual, direction)]
    moved = [step0 * d + step1 * f for d, f in zip(direction, following)]
    last = [r - step1 * (i + damping * f) for r, i, f in zip(residual, image, following)]
    return weights + jnp.concatenate(moved, axis=0), jnp.concatenate(last, axis=0)


def solution(mesh):
    in_specs = (P("clip", "feat"), P(None, "feat"), P("clip"))
    out_specs = (P(None, "feat"), P(None, "feat"))
    return jax.shard_map(local, mesh=mesh, in_specs=in_specs, out_specs=out_specs, check_vma=False)
```

```python
import functools

import jax
import jax.numpy as jnp
from jax import lax
from jax.experimental import pallas as pl
from jax.experimental.pallas import tpu as pltpu
from jax.sharding import PartitionSpec as P

damping = 0.01
F32, BF16 = jnp.float32, jnp.bfloat16
LANES, ROWS8, UNIT = 128, 8, 16
NT = (((1,), (1,)), ((), ()))
NN = (((1,), (0,)), ((), ()))
VMEM_LIMIT = 44 * 1024 * 1024


def parts_of(x):
    high = x.astype(BF16)
    return high, (x - high.astype(F32)).astype(BF16)


def dot3(x, high, low, dims):
    x_high, x_low = parts_of(x)
    dot = functools.partial(lax.dot_general, dimension_numbers=dims, preferred_element_type=F32)
    return dot(x_high, high) + (dot(x_low, high) + dot(x_high, low))


def params():
    return pltpu.CompilerParams(vmem_limit_bytes=VMEM_LIMIT)


class Plan:
    def __init__(self, rows, feats, classes, n_clip, n_feat):
        self.rows, self.feats, self.classes = rows, feats, classes
        self.n_clip, self.n_feat = n_clip, n_feat
        units = classes // UNIT
        sizes = [UNIT * (units // 4 + (k < units % 4)) for k in range(4)]
        starts = [sum(sizes[:k]) for k in range(4)]
        self.chunks = list(zip(starts, sizes))
        self.pairs = [(0, 1), (2, 3)]
        strides = [1 << k for k in range(1, n_clip.bit_length() - 1)]
        self.levels, block = [], feats
        while strides and block % (2 * LANES) == 0:
            self.levels.append(strides.pop(0))
            block //= 2
        self.doubled = strides
        self.block, self.nb = block, feats // block

    def pair_range(self, pair):
        first, last = self.pairs[pair][0], self.pairs[pair][-1]
        start = self.chunks[first][0]
        return start, self.chunks[last][0] + self.chunks[last][1] - start


def swap(x, axis, stride):
    size = lax.axis_size(axis)
    return lax.ppermute(x, axis, [(i, i ^ stride) for i in range(size)])


def first_body(plan, s_ref, f_ref, w_ref, high_ref, low_ref, *rest):
    outs, acc = rest[:-1], rest[-1]
    p = pl.program_id(0)
    high, low = parts_of(f_ref[...])
    high_ref[...] = high
    low_ref[...] = low
    part = dot3(w_ref[...], high, low, NT)

    @pl.when(p == 0)
    def _():
        acc[...] = part

    @pl.when(p > 0)
    def _():
        acc[...] += part

    @pl.when(p == plan.nb - 1)
    def _():
        halve(plan, s_ref, acc, outs, [(a, n) for a, n in plan.chunks])


def halve(plan, s_ref, acc, outs, ranges):
    half = plan.rows // 2
    bit = s_ref[2]
    keep = pl.multiple_of(bit * half, LANES)
    send = pl.multiple_of((1 - bit) * half, LANES)
    for k, (a, n) in enumerate(ranges):
        outs[2 * k][...] = acc[a : a + n, pl.ds(send, half)]
        outs[2 * k + 1][...] = acc[a : a + n, pl.ds(keep, half)]


def first(plan, where, features, weights):
    rows, block = plan.rows, plan.block
    half = rows // 2
    outs = [jax.ShapeDtypeStruct((rows, plan.feats), BF16)] * 2
    specs = [pl.BlockSpec((rows, block), lambda p, s: (0, p))] * 2
    for _, n in plan.chunks:
        outs += [jax.ShapeDtypeStruct((n, half), F32)] * 2
        specs += [pl.BlockSpec((n, half), lambda p, s: (0, 0))] * 2
    result = pl.pallas_call(
        functools.partial(first_body, plan),
        out_shape=outs,
        grid_spec=pltpu.PrefetchScalarGridSpec(
            num_scalar_prefetch=1,
            grid=(plan.nb,),
            in_specs=[
                pl.BlockSpec((rows, block), lambda p, s: (0, p ^ s[0])),
                pl.BlockSpec((plan.classes, block), lambda p, s: (0, p ^ s[0])),
            ],
            out_specs=specs,
            scratch_shapes=[pltpu.VMEM((plan.classes, rows), F32)],
        ),
        compiler_params=params(),
        name="split_and_logits",
    )(where, features, weights)
    return result[0], result[1], [tuple(result[2 + 2 * k : 4 + 2 * k]) for k in range(4)]


def back_body(plan, pair, s_ref, g_ref, high_ref, low_ref, *rest):
    outs, acc = rest[:-1], rest[-1]
    acc[...] = dot3(g_ref[...], high_ref[...], low_ref[...], NN)
    core = s_ref[1]
    base = plan.pair_range(pair)[0]
    for k, c in enumerate(plan.pairs[pair]):
        a, n = plan.chunks[c]
        h = n // 2
        outs[2 * k][...] = acc[pl.ds(pl.multiple_of(a - base + core * h, ROWS8), h), :]
        outs[2 * k + 1][...] = acc[pl.ds(pl.multiple_of(a - base + (1 - core) * h, ROWS8), h), :]


def back(plan, where, pair, values, high, low):
    rows, block, feats = plan.rows, plan.block, plan.feats
    n_pair = plan.pair_range(pair)[1]
    outs, specs = [], []
    for c in plan.pairs[pair]:
        h = plan.chunks[c][1] // 2
        outs += [jax.ShapeDtypeStruct((h, feats), F32)] * 2
        specs += [pl.BlockSpec((h, block), lambda p, s: (0, p))] * 2
    result = pl.pallas_call(
        functools.partial(back_body, plan, pair),
        out_shape=outs,
        grid_spec=pltpu.PrefetchScalarGridSpec(
            num_scalar_prefetch=1,
            grid=(plan.nb,),
            in_specs=[
                pl.BlockSpec((n_pair, rows), lambda p, s: (0, 0)),
                pl.BlockSpec((rows, block), lambda p, s: (0, p)),
                pl.BlockSpec((rows, block), lambda p, s: (0, p)),
            ],
            out_specs=specs,
            scratch_shapes=[pltpu.VMEM((n_pair, block), F32)],
        ),
        compiler_params=params(),
        cost_estimate=pl.CostEstimate(
            flops=6 * n_pair * rows * feats, bytes_accessed=4 * feats * (rows + n_pair), transcendentals=0
        ),
        name="back_pair",
    )(where, values, high, low)
    return [tuple(result[2 * k : 2 * k + 2]) for k in range(len(plan.pairs[pair]))]


def gather_rows(plan, pair, s_ref, pieces, position, target):
    core = s_ref[1]
    base = plan.pair_range(pair)[0]
    for k, c in enumerate(plan.pairs[pair]):
        a, n = plan.chunks[c]
        h = n // 2
        own, other = pieces[2 * k][position], pieces[2 * k + 1][position]
        target[pl.ds(pl.multiple_of(a - base + core * h, ROWS8), h), :] = own[...]
        target[pl.ds(pl.multiple_of(a - base + (1 - core) * h, ROWS8), h), :] = other[...]


def forth_body(plan, pair, step, s_ref, *refs):
    nb, n_chunks = plan.nb, len(plan.pairs[pair])
    n_pieces = 2 * n_chunks * nb
    refs = list(refs)
    scalar_ref = refs.pop(0) if step else None
    pieces = [refs[k * nb : (k + 1) * nb] for k in range(2 * n_chunks)]
    refs = refs[n_pieces:]
    direction_ref = refs.pop(0) if step else None
    high_ref, low_ref, vector_ref = refs[:3]
    outs, (target, acc, sums) = refs[3:-3], refs[-3:]
    base, n_pair = plan.pair_range(pair)
    p = pl.program_id(0)
    for position in range(nb):

        @pl.when(p == position)
        def _():
            gather_rows(plan, pair, s_ref, pieces, position, target)

    if step:
        direction = direction_ref[...]
        vector = direction - scalar_ref[0] * (target[...] + damping * direction)
    else:
        vector = -target[...]
    vector_ref[...] = vector
    part = dot3(vector, high_ref[...], low_ref[...], NT)
    square = jnp.sum(vector * vector).reshape(1, 1)
    cross = jnp.sum(vector * direction).reshape(1, 1) if step else square
    ids = lax.broadcasted_iota(jnp.int32, (ROWS8, plan.rows), 0)
    new = jnp.where(ids == 0, square, jnp.where(ids == 1, cross, 0.0))

    @pl.when(p == 0)
    def _():
        acc[:n_pair, :] = part
        sums[...] = new

    @pl.when(p > 0)
    def _():
        acc[:n_pair, :] += part
        sums[...] += new

    @pl.when(p == nb - 1)
    def _():
        acc[n_pair:, :] = sums[...]
        halve(plan, s_ref, acc, outs, tangent_ranges(plan, pair))


def tangent_ranges(plan, pair):
    base = plan.pair_range(pair)[0]
    ranges = [(plan.chunks[c][0] - base, plan.chunks[c][1]) for c in plan.pairs[pair]]
    ranges[-1] = (ranges[-1][0], ranges[-1][1] + ROWS8)
    return ranges


def forth(plan, where, pair, pieces, high, low, step=None, direction=None):
    rows, block, feats, nb = plan.rows, plan.block, plan.feats, plan.nb
    half = rows // 2
    n_pair = plan.pair_range(pair)[1]
    operands, in_specs = [], []
    if step is not None:
        operands.append(step.reshape(1))
        in_specs.append(pl.BlockSpec(memory_space=pltpu.SMEM))
    for own, other in pieces:
        for side in (own, other):
            for piece in side:
                operands.append(piece)
                in_specs.append(pl.BlockSpec(piece.shape, lambda p, s: (0, 0)))
    placed = pl.BlockSpec((n_pair, block), lambda p, s: (0, p ^ s[0]))
    if step is not None:
        operands.append(direction)
        in_specs.append(placed)
    operands += [high, low]
    in_specs += [pl.BlockSpec((rows, block), lambda p, s: (0, p))] * 2
    outs, specs = [jax.ShapeDtypeStruct((n_pair, feats), F32)], [placed]
    for _, n in tangent_ranges(plan, pair):
        outs += [jax.ShapeDtypeStruct((n, half), F32)] * 2
        specs += [pl.BlockSpec((n, half), lambda p, s: (0, 0))] * 2
    result = pl.pallas_call(
        functools.partial(forth_body, plan, pair, step is not None),
        out_shape=outs,
        grid_spec=pltpu.PrefetchScalarGridSpec(
            num_scalar_prefetch=1,
            grid=(nb,),
            in_specs=in_specs,
            out_specs=specs,
            scratch_shapes=[
                pltpu.VMEM((n_pair, block), F32),
                pltpu.VMEM((n_pair + ROWS8, rows), F32),
                pltpu.VMEM((ROWS8, rows), F32),
            ],
        ),
        compiler_params=params(),
        cost_estimate=pl.CostEstimate(
            flops=6 * n_pair * rows * feats, bytes_accessed=4 * feats * (rows + 3 * n_pair), transcendentals=0
        ),
        name="forth_pair",
    )(where, *operands)
    return result[0], [tuple(result[1 + 2 * k : 3 + 2 * k]) for k in range(len(plan.pairs[pair]))]


def last_body(plan, pair, s_ref, scalar_ref, *refs):
    nb, n_chunks = plan.nb, len(plan.pairs[pair])
    refs = list(refs)
    pieces = [refs[k * nb : (k + 1) * nb] for k in range(2 * n_chunks)]
    refs = refs[2 * n_chunks * nb :]
    direction_ref, residual_ref = refs[:2]
    out_ref, target, ready, sem = refs[-4:]
    base, n_pair = plan.pair_range(pair)
    p = pl.program_id(0)
    for position in range(nb):

        @pl.when(p == position)
        def _():
            gather_rows(plan, pair, s_ref, pieces, position, target)

    residual = residual_ref[...]
    following = residual + scalar_ref[1] * direction_ref[...]
    ready[...] = residual - scalar_ref[0] * (target[...] + damping * following)
    column = pl.multiple_of((p ^ s_ref[0]) * plan.block, LANES)
    copy = pltpu.make_async_copy(ready, out_ref.at[pl.ds(base, n_pair), pl.ds(column, plan.block)], sem)
    copy.start()
    copy.wait()


def last(plan, where, pair, scalars, pieces, direction, residual, out):
    block, nb = plan.block, plan.nb
    n_pair = plan.pair_range(pair)[1]
    operands, in_specs = [scalars], [pl.BlockSpec(memory_space=pltpu.SMEM)]
    for own, other in pieces:
        for side in (own, other):
            for piece in side:
                operands.append(piece)
                in_specs.append(pl.BlockSpec(piece.shape, lambda p, s: (0, 0)))
    operands += [direction, residual]
    in_specs += [pl.BlockSpec((n_pair, block), lambda p, s: (0, p ^ s[0]))] * 2
    aliases = {}
    if out is not None:
        aliases = {len(operands) + 1: 0}
        operands.append(out)
        in_specs.append(pl.BlockSpec(memory_space=pl.ANY))
    return pl.pallas_call(
        functools.partial(last_body, plan, pair),
        out_shape=jax.ShapeDtypeStruct((plan.classes, plan.feats), F32),
        grid_spec=pltpu.PrefetchScalarGridSpec(
            num_scalar_prefetch=1,
            grid=(nb,),
            in_specs=in_specs,
            out_specs=pl.BlockSpec(memory_space=pl.ANY),
            scratch_shapes=[
                pltpu.VMEM((n_pair, block), F32),
                pltpu.VMEM((n_pair, block), F32),
                pltpu.SemaphoreType.DMA,
            ],
        ),
        input_output_aliases=aliases,
        compiler_params=params(),
        cost_estimate=pl.CostEstimate(
            flops=6 * n_pair * plan.feats, bytes_accessed=16 * n_pair * plan.feats, transcendentals=0
        ),
        name="last_pair",
    )(where, *operands)


def sum_clip(plan, own, other, order):
    if plan.n_clip > 1:
        got = swap(other, "clip", 1)
        own = own + got
    blocks = {p: own[:, p * plan.block : (p + 1) * plan.block] for p in range(plan.nb)}
    levels = [(plan.levels[k], 1 << k) for k in range(len(plan.levels))]
    if order:
        levels = levels[::-1]
    active = list(range(plan.nb))
    for stride, bit in levels:
        rest = [p for p in active if not p & bit]
        got = {p: swap(blocks[p | bit], "clip", stride) for p in reversed(rest)}
        for p in reversed(rest):
            blocks[p] = blocks[p] + got[p]
        active = rest
    for stride in plan.doubled:
        blocks[0] = blocks[0] + swap(blocks[0], "clip", stride)
    for stride, bit in levels[::-1]:
        for p in active:
            blocks[p | bit] = swap(blocks[p], "clip", stride)
        active = active + [p | bit for p in active]
    mine = [blocks[p] for p in range(plan.nb)]
    theirs = [swap(b, "clip", 1) for b in mine] if plan.n_clip > 1 else mine
    return mine, theirs


def sum_feat(plan, halves, bit):
    send, keep = halves
    if plan.n_feat == 1:
        return jnp.where(bit, jnp.concatenate([send, keep], 1), jnp.concatenate([keep, send], 1))
    total = keep + swap(send, "feat", 1)
    stride = 2
    while stride < plan.n_feat:
        total = total + swap(total, "feat", stride)
        stride *= 2
    away = swap(total, "feat", 1)
    return jnp.where(bit, jnp.concatenate([away, total], 1), jnp.concatenate([total, away], 1))


def sum_clip_scalar(plan, value):
    row = jnp.broadcast_to(value, (ROWS8, LANES))
    stride = 1
    while stride < plan.n_clip:
        row = row + swap(row, "clip", stride)
        stride *= 2
    return row[0, 0]


def local(features, weights, labels):
    rows, feats = features.shape
    classes = weights.shape[0]
    plan = Plan(rows, feats, classes, lax.axis_size("clip"), lax.axis_size("feat"))
    total_rows = rows * plan.n_clip
    me, bit = lax.axis_index("clip"), lax.axis_index("feat") & 1
    mask = sum(((me // stride) & 1) << k for k, stride in enumerate(plan.levels))
    where = jnp.stack([jnp.asarray(mask), me & 1, bit]).astype(jnp.int32)

    high, low, halves = first(plan, where, features, weights)
    logits = jnp.concatenate([sum_feat(plan, pair, bit) for pair in halves], axis=0)
    top = jnp.max(logits, axis=0, keepdims=True)
    powers = jnp.exp(logits - top)
    probs = powers / jnp.sum(powers, axis=0, keepdims=True)
    onehot = (labels[None, :] == jnp.arange(classes, dtype=jnp.int32)[:, None]).astype(F32)

    def backward(values):
        result = []
        for pair in range(len(plan.pairs)):
            a, n = plan.pair_range(pair)
            sides = back(plan, where, pair, values[a : a + n], high, low)
            result.append([sum_clip(plan, own, other, k % 2) for k, (own, other) in enumerate(sides)])
        return result

    def forward(pieces, step=None, direction=None):
        vectors, tangents, sums = [], [], 0.0
        for pair in range(len(plan.pairs)):
            vector, halves = forth(
                plan, where, pair, pieces[pair], high, low, step, None if step is None else direction[pair]
            )
            vectors.append(vector)
            found = [sum_feat(plan, half, bit) for half in halves]
            n = plan.chunks[plan.pairs[pair][-1]][1]
            sums = sums + found[-1][n : n + 2, 0]
            found[-1] = found[-1][:n]
            tangents += found
        return vectors, jnp.concatenate(tangents, axis=0), sums

    def bend(tangent):
        weighted = probs * tangent
        bent = (weighted - probs * jnp.sum(weighted, axis=0, keepdims=True)) / total_rows
        return bent, sum_clip_scalar(plan, jnp.sum(bent * tangent))

    pieces = backward((probs - onehot) / total_rows)
    direction, tangent, sums = forward(pieces)
    norm0 = sums[0]
    bent, curvature = bend(tangent)
    step0 = norm0 / (curvature + damping * norm0)

    pieces = backward(bent)
    residual, fresh, sums = forward(pieces, step0, direction)
    norm1, cross = sums[0], sums[1]
    ratio = norm1 / norm0
    bent, curvature = bend(fresh + ratio * tangent)
    length = norm1 + 2.0 * ratio * cross + ratio * ratio * norm0
    step1 = norm1 / (curvature + damping * length)

    pieces = backward(bent)
    along = jnp.concatenate(direction, axis=0)
    moved = weights + (step0 + step1 * ratio) * along + step1 * jnp.concatenate(residual, axis=0)
    scalars = jnp.stack([step1, ratio])
    out = None
    for pair in range(len(plan.pairs)):
        out = last(plan, where, pair, scalars, pieces[pair], direction[pair], residual[pair], out)
    return moved, out


def solution(mesh):
    in_specs = (P("clip", "feat"), P(None, "feat"), P("clip"))
    out_specs = (P(None, "feat"), P(None, "feat"))
    return jax.shard_map(local, mesh=mesh, in_specs=in_specs, out_specs=out_specs, check_vma=False)
```

```python
import functools

import jax
import jax.numpy as jnp
from jax import lax
from jax.experimental import pallas as pl
from jax.experimental.pallas import tpu as pltpu
from jax.sharding import PartitionSpec as P

damping = 0.01
F32, BF16 = jnp.float32, jnp.bfloat16
LANES, ROWS8, UNIT = 128, 8, 16
NT = (((1,), (1,)), ((), ()))
NN = (((1,), (0,)), ((), ()))
VMEM_LIMIT = 52 * 1024 * 1024


def parts_of(x):
    high = x.astype(BF16)
    return high, (x - high.astype(F32)).astype(BF16)


def dot3(x, high, low, dims):
    x_high, x_low = parts_of(x)
    n = x.shape[0]
    dot = functools.partial(lax.dot_general, dimension_numbers=dims, preferred_element_type=F32)
    both = dot(jnp.concatenate([x_high, x_low], axis=0), high)
    return both[:n] + (both[n:] + dot(x_high, low))


def dot3_stream(high, low, x):
    x_high, x_low = parts_of(x)
    dot = functools.partial(lax.dot_general, dimension_numbers=NT, preferred_element_type=F32)
    return dot(high, x_high) + (dot(high, x_low) + dot(low, x_high))


def params():
    return pltpu.CompilerParams(vmem_limit_bytes=VMEM_LIMIT)


class Plan:
    def __init__(self, rows, feats, classes, n_clip, n_feat):
        self.rows, self.feats, self.classes = rows, feats, classes
        self.n_clip, self.n_feat = n_clip, n_feat
        units = classes // UNIT
        sizes = [UNIT * (units // 4 + (k < units % 4)) for k in range(4)]
        starts = [sum(sizes[:k]) for k in range(4)]
        self.chunks = list(zip(starts, sizes))
        self.pairs = [(0, 1), (2, 3)]
        strides = [1 << k for k in range(1, n_clip.bit_length() - 1)]
        self.levels, block = [], feats
        while strides and block % (2 * LANES) == 0:
            self.levels.append(strides.pop(0))
            block //= 2
        self.doubled = strides
        self.block, self.nb = block, feats // block
        self.rows_step = next(n for n in (256, 128, rows) if rows % n == 0)

    def pair_range(self, pair):
        first, last = self.pairs[pair][0], self.pairs[pair][-1]
        start = self.chunks[first][0]
        return start, self.chunks[last][0] + self.chunks[last][1] - start


def swap(x, axis, stride):
    size = lax.axis_size(axis)
    return lax.ppermute(x, axis, [(i, i ^ stride) for i in range(size)])


def first_body(plan, s_ref, f_ref, w_ref, *rest):
    high_ref, low_ref, send_ref, keep_ref, acc = rest[-5:]
    p = pl.program_id(0)
    high, low = parts_of(f_ref[...])
    high_ref[...] = high
    low_ref[...] = low
    part = dot3(w_ref[...], high, low, NT)

    @pl.when(p == 0)
    def _():
        acc[...] = part

    @pl.when(p > 0)
    def _():
        acc[...] += part

    @pl.when(p == plan.nb - 1)
    def _():
        half = plan.classes // 2
        bit = s_ref[2]
        send_ref[...] = acc[pl.ds(pl.multiple_of((1 - bit) * half, ROWS8), half), :]
        keep_ref[...] = acc[pl.ds(pl.multiple_of(bit * half, ROWS8), half), :]


def first(plan, where, features, weights, part, split):
    rows, block, step = plan.rows, plan.block, plan.rows_step
    half = plan.classes // 2
    operands = [features, weights]
    in_specs = [
        pl.BlockSpec((step, block), lambda p, s: (part, p ^ s[0])),
        pl.BlockSpec((plan.classes, block), lambda p, s: (0, p ^ s[0])),
    ]
    aliases = {}
    if split is not None:
        aliases = {3: 0, 4: 1}
        operands += list(split)
        in_specs += [pl.BlockSpec(memory_space=pl.ANY)] * 2
    high, low, send, keep = pl.pallas_call(
        functools.partial(first_body, plan),
        out_shape=[jax.ShapeDtypeStruct((rows, plan.feats), BF16)] * 2
        + [jax.ShapeDtypeStruct((half, step), F32)] * 2,
        grid_spec=pltpu.PrefetchScalarGridSpec(
            num_scalar_prefetch=1,
            grid=(plan.nb,),
            in_specs=in_specs,
            out_specs=[pl.BlockSpec((step, block), lambda p, s: (part, p))] * 2
            + [pl.BlockSpec((half, step), lambda p, s: (0, 0))] * 2,
            scratch_shapes=[pltpu.VMEM((plan.classes, step), F32)],
        ),
        input_output_aliases=aliases,
        compiler_params=params(),
        cost_estimate=pl.CostEstimate(
            flops=6 * plan.classes * step * plan.feats,
            bytes_accessed=4 * plan.feats * (2 * step + plan.classes),
            transcendentals=0,
        ),
        name="split_and_logits",
    )(where, *operands)
    return (high, low), (send, keep)


def back_body(plan, pair, s_ref, g_ref, high_ref, low_ref, *rest):
    outs, acc = rest[:-1], rest[-1]
    acc[...] = dot3(g_ref[...], high_ref[...], low_ref[...], NN)
    core = s_ref[1]
    base = plan.pair_range(pair)[0]
    for k, c in enumerate(plan.pairs[pair]):
        a, n = plan.chunks[c]
        h = n // 2
        outs[2 * k][...] = acc[pl.ds(pl.multiple_of(a - base + core * h, ROWS8), h), :]
        outs[2 * k + 1][...] = acc[pl.ds(pl.multiple_of(a - base + (1 - core) * h, ROWS8), h), :]


def back(plan, where, pair, values, high, low):
    rows, block, feats = plan.rows, plan.block, plan.feats
    n_pair = plan.pair_range(pair)[1]
    outs, specs = [], []
    for c in plan.pairs[pair]:
        h = plan.chunks[c][1] // 2
        outs += [jax.ShapeDtypeStruct((h, feats), F32)] * 2
        specs += [pl.BlockSpec((h, block), lambda p, s: (0, p))] * 2
    result = pl.pallas_call(
        functools.partial(back_body, plan, pair),
        out_shape=outs,
        grid_spec=pltpu.PrefetchScalarGridSpec(
            num_scalar_prefetch=1,
            grid=(plan.nb,),
            in_specs=[
                pl.BlockSpec((n_pair, rows), lambda p, s: (0, 0)),
                pl.BlockSpec((rows, block), lambda p, s: (0, p)),
                pl.BlockSpec((rows, block), lambda p, s: (0, p)),
            ],
            out_specs=specs,
            scratch_shapes=[pltpu.VMEM((n_pair, block), F32)],
        ),
        compiler_params=params(),
        cost_estimate=pl.CostEstimate(
            flops=6 * n_pair * rows * feats, bytes_accessed=4 * feats * (rows + n_pair), transcendentals=0
        ),
        name="back_pair",
    )(where, values, high, low)
    return [tuple(result[2 * k : 2 * k + 2]) for k in range(len(plan.pairs[pair]))]


class Pieces:
    def __init__(self, places, mine, theirs):
        self.places, self.mine, self.theirs = places, mine, theirs

    def flat(self):
        return list(self.mine) + list(self.theirs)


def gather_rows(plan, pair, chunks, s_ref, refs, position, target):
    core = s_ref[1]
    base = plan.pair_range(pair)[0]
    refs = list(refs)
    for c, places in zip(plan.pairs[pair], chunks):
        a, n = plan.chunks[c]
        h = n // 2
        for side in (core, 1 - core):
            for place in places:
                ref = refs.pop(0)
                if position in place:
                    k = place.index(position) * plan.block
                    target[pl.ds(pl.multiple_of(a - base + side * h, ROWS8), h), :] = ref[:, k : k + plan.block]


def forth_body(plan, pair, step, chunks, s_ref, *refs):
    nb = plan.nb
    refs = list(refs)
    scalar_ref = refs.pop(0) if step else None
    n_pieces = 2 * sum(len(places) for places in chunks)
    pieces, refs = refs[:n_pieces], refs[n_pieces:]
    direction_ref = refs.pop(0) if step else None
    high_ref, low_ref = refs[:2]
    n_ranges = len(tangent_ranges(plan, pair))
    target, acc, turned, sums = refs[-4:]
    vector_ref, outs = refs[-5 - 2 * n_ranges], refs[-4 - 2 * n_ranges : -4]
    n_pair = plan.pair_range(pair)[1]
    p = pl.program_id(0)
    for position in range(nb):

        @pl.when(p == position)
        def _():
            gather_rows(plan, pair, chunks, s_ref, pieces, position, target)

    if step:
        direction = direction_ref[...]
        vector = direction - scalar_ref[0] * (target[...] + damping * direction)
    else:
        vector = -target[...]
    vector_ref[...] = vector
    part = dot3_stream(high_ref[...], low_ref[...], vector)
    square = jnp.sum(vector * vector).reshape(1, 1)
    cross = jnp.sum(vector * direction).reshape(1, 1) if step else square
    ids = lax.broadcasted_iota(jnp.int32, (ROWS8, plan.rows), 0)
    new = jnp.where(ids == 0, square, jnp.where(ids == 1, cross, 0.0))

    @pl.when(p == 0)
    def _():
        acc[...] = part
        sums[...] = new

    @pl.when(p > 0)
    def _():
        acc[...] += part
        sums[...] += new

    @pl.when(p == nb - 1)
    def _():
        turned[:n_pair, :] = acc[...].T
        turned[n_pair:, :] = sums[...]
        half = plan.rows // 2
        bit = s_ref[2]
        keep = pl.multiple_of(bit * half, LANES)
        send = pl.multiple_of((1 - bit) * half, LANES)
        for k, (a, n) in enumerate(tangent_ranges(plan, pair)):
            outs[2 * k][...] = turned[a : a + n, pl.ds(send, half)]
            outs[2 * k + 1][...] = turned[a : a + n, pl.ds(keep, half)]


def tangent_ranges(plan, pair):
    base, n_pair = plan.pair_range(pair)
    if pair == 0:
        return [(0, n_pair + ROWS8)]
    ranges = [(plan.chunks[c][0] - base, plan.chunks[c][1]) for c in plan.pairs[pair]]
    ranges[-1] = (ranges[-1][0], ranges[-1][1] + ROWS8)
    return ranges


def placed(plan, pair):
    base, n_pair = plan.pair_range(pair)
    return pl.BlockSpec(
        (pl.Element(n_pair), pl.Element(plan.block)), lambda p, s: (base, (p ^ s[0]) * plan.block)
    )


def forth(plan, where, pair, pieces, high, low, vectors, step=None, direction=None):
    rows, block, feats, nb = plan.rows, plan.block, plan.feats, plan.nb
    half = rows // 2
    n_pair = plan.pair_range(pair)[1]
    operands, in_specs = [], []
    if step is not None:
        operands.append(step.reshape(1))
        in_specs.append(pl.BlockSpec(memory_space=pltpu.SMEM))
    for piece in pieces:
        for x in piece.flat():
            operands.append(x)
            in_specs.append(pl.BlockSpec(x.shape, lambda p, s: (0, 0)))
    if step is not None:
        operands.append(direction)
        in_specs.append(placed(plan, pair))
    operands += [high, low]
    in_specs += [pl.BlockSpec((rows, block), lambda p, s: (0, p))] * 2
    aliases = {}
    if vectors is not None:
        aliases = {len(operands) + 1: 0}
        operands.append(vectors)
        in_specs.append(pl.BlockSpec(memory_space=pl.ANY))
    outs, specs = [jax.ShapeDtypeStruct((plan.classes, feats), F32)], [placed(plan, pair)]
    for _, n in tangent_ranges(plan, pair):
        outs += [jax.ShapeDtypeStruct((n, half), F32)] * 2
        specs += [pl.BlockSpec((n, half), lambda p, s: (0, 0))] * 2
    result = pl.pallas_call(
        functools.partial(forth_body, plan, pair, step is not None, [piece.places for piece in pieces]),
        out_shape=outs,
        grid_spec=pltpu.PrefetchScalarGridSpec(
            num_scalar_prefetch=1,
            grid=(nb,),
            in_specs=in_specs,
            out_specs=specs,
            scratch_shapes=[
                pltpu.VMEM((n_pair, block), F32),
                pltpu.VMEM((rows, n_pair), F32),
                pltpu.VMEM((n_pair + ROWS8, rows), F32),
                pltpu.VMEM((ROWS8, rows), F32),
            ],
        ),
        input_output_aliases=aliases,
        compiler_params=params(),
        cost_estimate=pl.CostEstimate(
            flops=6 * n_pair * rows * feats, bytes_accessed=4 * feats * (rows + 3 * n_pair), transcendentals=0
        ),
        name="forth_pair",
    )(where, *operands)
    return result[0], [tuple(result[1 + 2 * k : 3 + 2 * k]) for k in range(len(tangent_ranges(plan, pair)))]


def last_body(plan, pair, chunks, s_ref, scalar_ref, *refs):
    nb = plan.nb
    refs = list(refs)
    n_pieces = 2 * sum(len(places) for places in chunks)
    pieces = refs[:n_pieces]
    base_ref, out_ref, target, ready, arrived, left = refs[n_pieces:]
    base, n_pair = plan.pair_range(pair)

    def place(ref, position):
        column = pl.multiple_of((position ^ s_ref[0]) * plan.block, LANES)
        return ref.at[pl.ds(base, n_pair), pl.ds(column, plan.block)]

    reads = [
        pltpu.make_async_copy(place(base_ref, q), ready.at[q], arrived.at[q]) for q in range(nb)
    ]
    writes = [pltpu.make_async_copy(ready.at[q], place(out_ref, q), left.at[q]) for q in range(nb)]
    for read in reads:
        read.start()
    for position in range(nb):
        gather_rows(plan, pair, chunks, s_ref, pieces, position, target)
        reads[position].wait()
        ready[position] = ready[position] - scalar_ref[0] * target[...]
        writes[position].start()
    for write in writes:
        write.wait()


def last(plan, where, pair, step, pieces, base):
    block, nb = plan.block, plan.nb
    n_pair = plan.pair_range(pair)[1]
    operands, in_specs = [where, step.reshape(1)], [pl.BlockSpec(memory_space=pltpu.SMEM)] * 2
    for piece in pieces:
        for x in piece.flat():
            operands.append(x)
            in_specs.append(pl.BlockSpec(memory_space=pltpu.VMEM))
    operands.append(base)
    in_specs.append(pl.BlockSpec(memory_space=pl.ANY))
    return pl.pallas_call(
        functools.partial(last_body, plan, pair, [piece.places for piece in pieces]),
        out_shape=jax.ShapeDtypeStruct((plan.classes, plan.feats), F32),
        in_specs=in_specs,
        out_specs=pl.BlockSpec(memory_space=pl.ANY),
        scratch_shapes=[
            pltpu.VMEM((n_pair, block), F32),
            pltpu.VMEM((nb, n_pair, block), F32),
            pltpu.SemaphoreType.DMA((nb,)),
            pltpu.SemaphoreType.DMA((nb,)),
        ],
        input_output_aliases={len(operands) - 1: 0},
        compiler_params=params(),
        cost_estimate=pl.CostEstimate(
            flops=6 * n_pair * plan.feats, bytes_accessed=12 * n_pair * plan.feats, transcendentals=0
        ),
        name="last_pair",
    )(*operands)


def tie(*values):
    return lax.optimization_barrier(values)


def columns(plan, x, positions):
    if list(positions) == list(range(positions[0], positions[-1] + 1)):
        return x[:, positions[0] * plan.block : (positions[-1] + 1) * plan.block]
    return jnp.concatenate([x[:, p * plan.block : (p + 1) * plan.block] for p in positions], axis=1)


class ClipSum:
    def __init__(self, plan, sides, order):
        self.plan = plan
        self.own, self.other = sides
        levels = [(plan.levels[k], 1 << k) for k in range(len(plan.levels))]
        self.levels = levels[::-1] if order else levels

    def cores(self):
        if self.plan.n_clip > 1:
            self.own = self.own + swap(self.other, "clip", 1)
        self.active = list(range(self.plan.nb))

    def scatter(self, k):
        stride, bit = self.levels[k]
        rest = [p for p in self.active if not p & bit]
        sent = columns(self.plan, self.own, [self.active.index(p | bit) for p in rest])
        kept = columns(self.plan, self.own, [self.active.index(p) for p in rest])
        self.own = kept + swap(sent, "clip", stride)
        self.active = rest

    def double(self):
        for stride in self.plan.doubled:
            self.own = self.own + swap(self.own, "clip", stride)
        self.places, self.mine = [tuple(self.active)], [self.own]

    def gather(self, k):
        stride, bit = self.levels[k]
        whole = self.mine[0] if len(self.mine) == 1 else jnp.concatenate(self.mine, axis=1)
        self.mine.append(swap(whole, "clip", stride))
        self.places.append(tuple(p | bit for place in self.places for p in place))

    def pieces(self):
        theirs = [swap(x, "clip", 1) for x in self.mine] if self.plan.n_clip > 1 else self.mine
        return Pieces(self.places, self.mine, theirs)


def sum_clips(plan, sides, value, during):
    sums = [ClipSum(plan, side, k % 2) for k, side in enumerate(sides)]
    for s in sums:
        s.cores()
    sums[0].own, value = tie(sums[0].own, value)
    result = during(value)
    steps = len(plan.levels)
    for k in range(steps):
        for s in sums:
            s.scatter(k)
        if k == steps - 1:
            sums[0].own, result = tie(sums[0].own, result)
    for s in sums:
        s.double()
    for k in reversed(range(steps)):
        for s in sums:
            s.gather(k)
    return sums, result


def sum_feat(plan, halves, bit, axis):
    send, keep = halves
    if plan.n_feat == 1:
        return jnp.where(bit, jnp.concatenate([send, keep], axis), jnp.concatenate([keep, send], axis))
    total = keep + swap(send, "feat", 1)
    stride = 2
    while stride < plan.n_feat:
        total = total + swap(total, "feat", stride)
        stride *= 2
    away = swap(total, "feat", 1)
    return jnp.where(bit, jnp.concatenate([away, total], axis), jnp.concatenate([total, away], axis))


def sum_clip_scalar(plan, value):
    row = jnp.broadcast_to(value, (ROWS8, LANES))
    stride = 1
    while stride < plan.n_clip:
        row = row + swap(row, "clip", stride)
        stride *= 2
    return row[0, 0]


def local(features, weights, labels):
    rows, feats = features.shape
    classes = weights.shape[0]
    plan = Plan(rows, feats, classes, lax.axis_size("clip"), lax.axis_size("feat"))
    total_rows = rows * plan.n_clip
    me, bit = lax.axis_index("clip"), lax.axis_index("feat") & 1
    mask = sum(((me // stride) & 1) << k for k, stride in enumerate(plan.levels))
    where = jnp.stack([jnp.asarray(mask), me & 1, bit]).astype(jnp.int32)

    split, parts = None, []
    for part in range(rows // plan.rows_step):
        split, halves = first(plan, where, features, weights, part, split)
        parts.append(halves)
    high, low = split
    probs, values = [], []
    for part, halves in enumerate(parts):
        logits = sum_feat(plan, halves, bit, 0)
        top = jnp.max(logits, axis=0, keepdims=True)
        powers = jnp.exp(logits - top)
        some = powers / jnp.sum(powers, axis=0, keepdims=True)
        mine = labels[part * plan.rows_step : (part + 1) * plan.rows_step]
        onehot = (mine[None, :] == jnp.arange(classes, dtype=jnp.int32)[:, None]).astype(F32)
        probs.append(some)
        values.append((some - onehot) / total_rows)
    probs, values = jnp.concatenate(probs, axis=1), jnp.concatenate(values, axis=1)

    def backward(values, value=0.0, during=lambda value: value):
        sides = []
        for pair in range(len(plan.pairs)):
            a, n = plan.pair_range(pair)
            sides += back(plan, where, pair, values[a : a + n], high, low)
        return sum_clips(plan, sides, jnp.asarray(value, F32), during)

    def forward(sums, step=None, direction=None):
        vectors, tangents, inner, ahead = None, [], 0.0, None
        for pair, members in enumerate(plan.pairs):
            if ahead is not None:
                for c in members:
                    sums[c].mine[-1], halves[0] = tie(sums[c].mine[-1], halves[0])
            if pair:
                tangents.append((pair - 1, halves))
            pieces = [sums[c].pieces() for c in members]
            vectors, halves = forth(plan, where, pair, pieces, high, low, vectors, step, direction)
            ahead = halves
        tangents.append((len(plan.pairs) - 1, halves))
        found = []
        for pair, halves in tangents:
            some = [sum_feat(plan, half, bit, 1) for half in halves]
            n = some[-1].shape[0] - ROWS8
            inner = inner + some[-1][n : n + 2, 0]
            some[-1] = some[-1][:n]
            found += some
        return vectors, jnp.concatenate(found, axis=0), inner

    def bend(tangent):
        weighted = probs * tangent
        bent = (weighted - probs * jnp.sum(weighted, axis=0, keepdims=True)) / total_rows
        return bent, jnp.sum(bent * tangent)

    sums, _ = backward(values)
    direction, tangent, inner = forward(sums)
    norm0 = inner[0]
    bent, curvature = bend(tangent)

    def first_step(curvature):
        return norm0 / (sum_clip_scalar(plan, curvature) + damping * norm0)

    sums, step0 = backward(bent, curvature, first_step)
    residual, fresh, inner = forward(sums, step0, direction)
    norm1, cross = inner[0], inner[1]
    ratio = norm1 / norm0
    bent, curvature = bend(fresh + ratio * tangent)
    length = norm1 + 2.0 * ratio * cross + ratio * ratio * norm0

    def second_step(curvature):
        step1 = norm1 / (sum_clip_scalar(plan, curvature) + damping * length)
        moved = weights + (step0 + step1 * ratio) * direction + step1 * residual
        base = residual - (step1 * damping) * (residual + ratio * direction)
        return step1, moved, base

    sums, (step1, moved, base) = backward(bent, curvature, second_step)
    for pair, members in enumerate(plan.pairs):
        base = last(plan, where, pair, step1, [sums[c].pieces() for c in members], base)
    return moved, base


def solution(mesh):
    in_specs = (P("clip", "feat"), P(None, "feat"), P("clip"))
    out_specs = (P(None, "feat"), P(None, "feat"))
    return jax.shard_map(local, mesh=mesh, in_specs=in_specs, out_specs=out_specs, check_vma=False)
```

```python
import functools

import jax
import jax.numpy as jnp
from jax import lax
from jax.experimental import pallas as pl
from jax.experimental.pallas import tpu as pltpu
from jax.sharding import PartitionSpec as P

damping = 0.01
F32, BF16 = jnp.float32, jnp.bfloat16
LANES, ROWS8, UNIT = 128, 8, 16
NT = (((1,), (1,)), ((), ()))
NN = (((1,), (0,)), ((), ()))
VMEM_LIMIT = 52 * 1024 * 1024


def parts_of(x):
    high = x.astype(BF16)
    return high, (x - high.astype(F32)).astype(BF16)


def dot3(x, high, low, dims):
    x_high, x_low = parts_of(x)
    dot = functools.partial(lax.dot_general, dimension_numbers=dims, preferred_element_type=F32)
    return dot(x_high, high) + (dot(x_low, high) + dot(x_high, low))


def params():
    return pltpu.CompilerParams(vmem_limit_bytes=VMEM_LIMIT)


class Plan:
    def __init__(self, rows, feats, classes, n_clip, n_feat):
        self.rows, self.feats, self.classes = rows, feats, classes
        self.n_clip, self.n_feat = n_clip, n_feat
        units = classes // UNIT
        sizes = [UNIT * (units // 4 + (k < units % 4)) for k in range(4)]
        starts = [sum(sizes[:k]) for k in range(4)]
        self.chunks = list(zip(starts, sizes))
        self.pairs = [(0,), (1, 2), (3,)]
        self.turns = [(0, 0), (1, 1), (0, 0), (0, 1)]
        strides = [1 << k for k in range(1, n_clip.bit_length() - 1)]
        self.levels, block = [], feats
        while strides and block % (2 * LANES) == 0:
            self.levels.append(strides.pop(0))
            block //= 2
        self.doubled = strides
        self.block, self.nb = block, feats // block
        self.rows_step = next(n for n in (384, 256, 128, rows) if rows % n == 0)

    def pair_range(self, pair):
        first, last = self.pairs[pair][0], self.pairs[pair][-1]
        start = self.chunks[first][0]
        return start, self.chunks[last][0] + self.chunks[last][1] - start


def swap(x, axis, stride):
    size = lax.axis_size(axis)
    return lax.ppermute(x, axis, [(i, i ^ stride) for i in range(size)])


def first_body(plan, s_ref, f_ref, w_ref, *rest):
    high_ref, low_ref, send_ref, keep_ref, acc = rest[-5:]
    p = pl.program_id(0)
    high, low = parts_of(f_ref[...])
    high_ref[...] = high
    low_ref[...] = low
    part = dot3(w_ref[...], high, low, NT)

    @pl.when(p == 0)
    def _():
        acc[...] = part

    @pl.when(p > 0)
    def _():
        acc[...] += part

    @pl.when(p == plan.nb - 1)
    def _():
        half = plan.classes // 2
        bit = s_ref[2]
        send_ref[...] = acc[pl.ds(pl.multiple_of((1 - bit) * half, ROWS8), half), :]
        keep_ref[...] = acc[pl.ds(pl.multiple_of(bit * half, ROWS8), half), :]


def first(plan, where, features, weights, part, split):
    rows, block, step = plan.rows, plan.block, plan.rows_step
    half = plan.classes // 2
    operands = [features, weights]
    in_specs = [
        pl.BlockSpec((step, block), lambda p, s: (part, p ^ s[0])),
        pl.BlockSpec((plan.classes, block), lambda p, s: (0, p ^ s[0])),
    ]
    aliases = {}
    if split is not None:
        aliases = {3: 0, 4: 1}
        operands += list(split)
        in_specs += [pl.BlockSpec(memory_space=pl.ANY)] * 2
    high, low, send, keep = pl.pallas_call(
        functools.partial(first_body, plan),
        out_shape=[jax.ShapeDtypeStruct((rows, plan.feats), BF16)] * 2
        + [jax.ShapeDtypeStruct((half, step), F32)] * 2,
        grid_spec=pltpu.PrefetchScalarGridSpec(
            num_scalar_prefetch=1,
            grid=(plan.nb,),
            in_specs=in_specs,
            out_specs=[pl.BlockSpec((step, block), lambda p, s: (part, p))] * 2
            + [pl.BlockSpec((half, step), lambda p, s: (0, 0))] * 2,
            scratch_shapes=[pltpu.VMEM((plan.classes, step), F32)],
        ),
        input_output_aliases=aliases,
        compiler_params=params(),
        cost_estimate=pl.CostEstimate(
            flops=6 * plan.classes * step * plan.feats,
            bytes_accessed=4 * plan.feats * (2 * step + plan.classes),
            transcendentals=0,
        ),
        name="split_and_logits",
    )(where, *operands)
    return (high, low), (send, keep)


def back_body(plan, pair, s_ref, g_ref, high_ref, low_ref, *outs):
    core = s_ref[1]
    base = plan.pair_range(pair)[0]
    some, ends = [], []
    for c in plan.pairs[pair]:
        a, n = plan.chunks[c]
        h = n // 2
        for side in (core, 1 - core):
            some.append(g_ref[pl.ds(pl.multiple_of(a - base + side * h, ROWS8), h), :])
            ends.append((ends[-1] if ends else 0) + h)
    x = jnp.concatenate(some, axis=0)
    width = 2 * LANES
    for k in range(0, plan.block, width):
        w = min(width, plan.block - k)
        part = dot3(x, high_ref[:, k : k + w], low_ref[:, k : k + w], NN)
        for out, start, end in zip(outs, [0] + ends, ends):
            out[:, k : k + w] = part[start:end]


def back(plan, where, pair, values, high, low):
    rows, block, feats = plan.rows, plan.block, plan.feats
    n_pair = plan.pair_range(pair)[1]
    outs, specs = [], []
    for c in plan.pairs[pair]:
        h = plan.chunks[c][1] // 2
        outs += [jax.ShapeDtypeStruct((h, feats), F32)] * 2
        specs += [pl.BlockSpec((h, block), lambda p, s: (0, p))] * 2
    result = pl.pallas_call(
        functools.partial(back_body, plan, pair),
        out_shape=outs,
        grid_spec=pltpu.PrefetchScalarGridSpec(
            num_scalar_prefetch=1,
            grid=(plan.nb,),
            in_specs=[
                pl.BlockSpec((n_pair, rows), lambda p, s: (0, 0)),
                pl.BlockSpec((rows, block), lambda p, s: (0, p)),
                pl.BlockSpec((rows, block), lambda p, s: (0, p)),
            ],
            out_specs=specs,
        ),
        compiler_params=params(),
        cost_estimate=pl.CostEstimate(
            flops=6 * n_pair * rows * feats, bytes_accessed=4 * feats * (rows + n_pair), transcendentals=0
        ),
        name="back_pair",
    )(where, values, high, low)
    return [tuple(result[2 * k : 2 * k + 2]) for k in range(len(plan.pairs[pair]))]


class Pieces:
    def __init__(self, places, mine, theirs):
        self.places = (places, [tuple(p for place in places for p in place)])
        self.mine, self.theirs = mine, theirs

    def flat(self):
        return list(self.mine) + [self.theirs]


def gather_rows(plan, pair, chunks, s_ref, refs, position, target):
    core = s_ref[1]
    base = plan.pair_range(pair)[0]
    refs = list(refs)
    for c, places in zip(plan.pairs[pair], chunks):
        a, n = plan.chunks[c]
        h = n // 2
        for side, some in zip((core, 1 - core), places):
            for place in some:
                ref = refs.pop(0)
                if position in place:
                    k = place.index(position) * plan.block
                    target[pl.ds(pl.multiple_of(a - base + side * h, ROWS8), h), :] = ref[:, k : k + plan.block]


def forth_body(plan, pair, step, chunks, s_ref, *refs):
    nb = plan.nb
    refs = list(refs)
    scalar_ref = refs.pop(0) if step else None
    n_pieces = sum(len(some) for places in chunks for some in places)
    pieces, refs = refs[:n_pieces], refs[n_pieces:]
    direction_ref = refs.pop(0) if step else None
    high_ref, low_ref = refs[:2]
    n_ranges = len(tangent_ranges(plan, pair))
    target, acc, sums = refs[-3:]
    vector_ref, outs = refs[-4 - 2 * n_ranges], refs[-3 - 2 * n_ranges : -3]
    n_pair = plan.pair_range(pair)[1]
    p = pl.program_id(0)
    for position in range(nb):

        @pl.when(p == position)
        def _():
            gather_rows(plan, pair, chunks, s_ref, pieces, position, target)

    if step:
        direction = direction_ref[...]
        vector = direction - scalar_ref[0] * (target[...] + damping * direction)
    else:
        vector = -target[...]
    vector_ref[...] = vector
    part = dot3(vector, high_ref[...], low_ref[...], NT)
    square = jnp.sum(vector * vector).reshape(1, 1)
    cross = jnp.sum(vector * direction).reshape(1, 1) if step else square
    ids = lax.broadcasted_iota(jnp.int32, (ROWS8, plan.rows), 0)
    new = jnp.where(ids == 0, square, jnp.where(ids == 1, cross, 0.0))

    @pl.when(p == 0)
    def _():
        acc[:n_pair, :] = part
        sums[...] = new

    @pl.when(p > 0)
    def _():
        acc[:n_pair, :] += part
        sums[...] += new

    @pl.when(p == nb - 1)
    def _():
        acc[n_pair:, :] = sums[...]
        half = plan.rows // 2
        bit = s_ref[2]
        keep = pl.multiple_of(bit * half, LANES)
        send = pl.multiple_of((1 - bit) * half, LANES)
        for k, (a, n) in enumerate(tangent_ranges(plan, pair)):
            outs[2 * k][...] = acc[a : a + n, pl.ds(send, half)]
            outs[2 * k + 1][...] = acc[a : a + n, pl.ds(keep, half)]


def tangent_ranges(plan, pair):
    return [(0, plan.pair_range(pair)[1] + ROWS8)]


def placed(plan, pair):
    base, n_pair = plan.pair_range(pair)
    return pl.BlockSpec(
        (pl.Element(n_pair), pl.Element(plan.block)), lambda p, s: (base, (p ^ s[0]) * plan.block)
    )


def forth(plan, where, pair, pieces, high, low, vectors, step=None, direction=None):
    rows, block, feats, nb = plan.rows, plan.block, plan.feats, plan.nb
    half = rows // 2
    n_pair = plan.pair_range(pair)[1]
    operands, in_specs = [], []
    if step is not None:
        operands.append(step.reshape(1))
        in_specs.append(pl.BlockSpec(memory_space=pltpu.SMEM))
    for piece in pieces:
        for x in piece.flat():
            operands.append(x)
            in_specs.append(pl.BlockSpec(x.shape, lambda p, s: (0, 0)))
    if step is not None:
        operands.append(direction)
        in_specs.append(placed(plan, pair))
    operands += [high, low]
    in_specs += [pl.BlockSpec((rows, block), lambda p, s: (0, p))] * 2
    aliases = {}
    if vectors is not None:
        aliases = {len(operands) + 1: 0}
        operands.append(vectors)
        in_specs.append(pl.BlockSpec(memory_space=pl.ANY))
    outs, specs = [jax.ShapeDtypeStruct((plan.classes, feats), F32)], [placed(plan, pair)]
    for _, n in tangent_ranges(plan, pair):
        outs += [jax.ShapeDtypeStruct((n, half), F32)] * 2
        specs += [pl.BlockSpec((n, half), lambda p, s: (0, 0))] * 2
    result = pl.pallas_call(
        functools.partial(forth_body, plan, pair, step is not None, [piece.places for piece in pieces]),
        out_shape=outs,
        grid_spec=pltpu.PrefetchScalarGridSpec(
            num_scalar_prefetch=1,
            grid=(nb,),
            in_specs=in_specs,
            out_specs=specs,
            scratch_shapes=[
                pltpu.VMEM((n_pair, block), F32),
                pltpu.VMEM((n_pair + ROWS8, rows), F32),
                pltpu.VMEM((ROWS8, rows), F32),
            ],
        ),
        input_output_aliases=aliases,
        compiler_params=params(),
        cost_estimate=pl.CostEstimate(
            flops=6 * n_pair * rows * feats, bytes_accessed=4 * feats * (rows + 3 * n_pair), transcendentals=0
        ),
        name="forth_pair",
    )(where, *operands)
    return result[0], [tuple(result[1 + 2 * k : 3 + 2 * k]) for k in range(len(tangent_ranges(plan, pair)))]


def last_body(plan, pair, chunks, s_ref, scalar_ref, *refs):
    nb = plan.nb
    refs = list(refs)
    n_pieces = sum(len(some) for places in chunks for some in places)
    pieces = refs[:n_pieces]
    direction_ref, residual_ref = refs[n_pieces : n_pieces + 2]
    out_ref, target, along, ready, arrived, left = refs[-6:]
    base, n_pair = plan.pair_range(pair)

    def place(ref, position):
        column = pl.multiple_of((position ^ s_ref[0]) * plan.block, LANES)
        return ref.at[pl.ds(base, n_pair), pl.ds(column, plan.block)]

    reads = []
    for q in range(nb):
        reads.append(pltpu.make_async_copy(place(direction_ref, q), along.at[q], arrived.at[0, q]))
        reads.append(pltpu.make_async_copy(place(residual_ref, q), ready.at[q], arrived.at[1, q]))
    writes = [pltpu.make_async_copy(ready.at[q], place(out_ref, q), left.at[q]) for q in range(nb)]
    for read in reads:
        read.start()
    for q in range(nb):
        gather_rows(plan, pair, chunks, s_ref, pieces, q, target)
        reads[2 * q].wait()
        reads[2 * q + 1].wait()
        residual = ready[q]
        following = residual + scalar_ref[1] * along[q]
        ready[q] = residual - scalar_ref[0] * (target[...] + damping * following)
        writes[q].start()
    for write in writes:
        write.wait()


def last(plan, where, pair, scalars, pieces, direction, residual, out):
    block, nb = plan.block, plan.nb
    n_pair = plan.pair_range(pair)[1]
    operands, in_specs = [where, scalars], [pl.BlockSpec(memory_space=pltpu.SMEM)] * 2
    for piece in pieces:
        for x in piece.flat():
            operands.append(x)
            in_specs.append(pl.BlockSpec(memory_space=pltpu.VMEM))
    operands += [direction, residual]
    aliases = {}
    if out is not None:
        aliases = {len(operands): 0}
        operands.append(out)
    in_specs += [pl.BlockSpec(memory_space=pl.ANY)] * (len(operands) - len(in_specs))
    return pl.pallas_call(
        functools.partial(last_body, plan, pair, [piece.places for piece in pieces]),
        out_shape=jax.ShapeDtypeStruct((plan.classes, plan.feats), F32),
        in_specs=in_specs,
        out_specs=pl.BlockSpec(memory_space=pl.ANY),
        scratch_shapes=[
            pltpu.VMEM((n_pair, block), F32),
            pltpu.VMEM((nb, n_pair, block), F32),
            pltpu.VMEM((nb, n_pair, block), F32),
            pltpu.SemaphoreType.DMA((2, nb)),
            pltpu.SemaphoreType.DMA((nb,)),
        ],
        input_output_aliases=aliases,
        compiler_params=params(),
        cost_estimate=pl.CostEstimate(
            flops=6 * n_pair * plan.feats, bytes_accessed=16 * n_pair * plan.feats, transcendentals=0
        ),
        name="last_rows",
    )(*operands)


class Order:
    def __init__(self):
        self.token = None

    def after(self, x):
        if self.token is None:
            return x
        return lax.optimization_barrier((x, self.token))[0]

    def note(self, x):
        self.token = x


def columns(plan, x, positions):
    if list(positions) == list(range(positions[0], positions[-1] + 1)):
        return x[:, positions[0] * plan.block : (positions[-1] + 1) * plan.block]
    return jnp.concatenate([x[:, p * plan.block : (p + 1) * plan.block] for p in positions], axis=1)


class ClipSum:
    def __init__(self, plan, sides, turns):
        self.plan = plan
        self.own, other = sides
        levels = [(stride, 1 << k) for k, stride in enumerate(plan.levels)]
        down, up = (levels[::-1] if turn else levels for turn in turns)
        self.active = list(range(plan.nb))
        self.places, self.mine = [], []
        self.steps = [("core", 1, 0)]
        self.steps += [("scatter", stride, bit) for stride, bit in down]
        self.steps += [("double", stride, 0) for stride in plan.doubled]
        self.steps += [("gather", stride, bit) for stride, bit in up]
        self.kept = self.own
        self.pending = swap(other, "clip", 1)

    def done(self):
        return not self.steps

    def advance(self, order):
        kind, _, bit = self.steps.pop(0)
        got = order.after(self.pending)
        if kind == "gather":
            self.mine.append(got)
            self.places.append(tuple(p | bit for place in self.places for p in place))
        else:
            self.own = self.kept + got
            if not self.steps or self.steps[0][0] == "gather":
                self.places, self.mine = [tuple(self.active)], [self.own]
        kind, stride, bit = self.steps[0] if self.steps else ("core", 1, 0)
        if kind == "scatter":
            rest = [p for p in self.active if not p & bit]
            sent = columns(self.plan, self.own, [self.active.index(p | bit) for p in rest])
            self.kept = columns(self.plan, self.own, [self.active.index(p) for p in rest])
            self.active = rest
        elif kind == "double":
            sent = self.kept = self.own
        else:
            sent = self.mine[0] if len(self.mine) == 1 else jnp.concatenate(self.mine, axis=1)
        order.note(sent)
        self.pending = swap(sent, "clip", stride)

    def pieces(self, order):
        while not self.done():
            self.advance(order)
        return Pieces(self.places, self.mine, order.after(self.pending))


class FeatSum:
    def __init__(self, plan, halves, bit, axis):
        send, self.kept = halves
        self.bit, self.axis = bit, axis
        strides = [1 << k for k in range(plan.n_feat.bit_length() - 1)]
        self.strides = strides + [1]
        self.pending = swap(send, "feat", 1)

    def advance(self, order):
        self.strides.pop(0)
        got = order.after(self.pending)
        if self.strides:
            self.kept = self.kept + got
            self.pending = swap(self.kept, "feat", self.strides[0])
            order.note(self.kept)
        else:
            self.got = got
            order.note(got)

    def result(self, order):
        while self.strides:
            self.advance(order)
        one, two = [self.got, self.kept], [self.kept, self.got]
        return jnp.where(self.bit, jnp.concatenate(one, self.axis), jnp.concatenate(two, self.axis))


class ScalarSum:
    def __init__(self, plan, value):
        self.strides = [1 << k for k in range(plan.n_clip.bit_length() - 1)]
        self.row = jnp.broadcast_to(value, (ROWS8, LANES))
        self.pending = swap(self.row, "clip", 1)

    def advance(self, order):
        if not self.strides:
            return
        self.strides.pop(0)
        self.row = self.row + order.after(self.pending)
        order.note(self.row)
        if self.strides:
            self.pending = swap(self.row, "clip", self.strides[0])

    def result(self, order):
        while self.strides:
            self.advance(order)
        return self.row[0, 0]


def local(features, weights, labels):
    rows, feats = features.shape
    classes = weights.shape[0]
    plan = Plan(rows, feats, classes, lax.axis_size("clip"), lax.axis_size("feat"))
    total_rows = rows * plan.n_clip
    me, bit = lax.axis_index("clip"), lax.axis_index("feat") & 1
    mask = sum(((me // stride) & 1) << k for k, stride in enumerate(plan.levels))
    where = jnp.stack([jnp.asarray(mask), me & 1, bit]).astype(jnp.int32)
    order = Order()
    groups = range(len(plan.pairs))

    split, parts = None, []
    for part in range(rows // plan.rows_step):
        split, halves = first(plan, where, features, weights, part, split)
        parts.append(FeatSum(plan, halves, bit, 0))
    high, low = split
    probs, values = [], []
    for part, summed in enumerate(parts):
        logits = summed.result(Order())
        top = jnp.max(logits, axis=0, keepdims=True)
        powers = jnp.exp(logits - top)
        some = powers / jnp.sum(powers, axis=0, keepdims=True)
        mine = labels[part * plan.rows_step : (part + 1) * plan.rows_step]
        onehot = (mine[None, :] == jnp.arange(classes, dtype=jnp.int32)[:, None]).astype(F32)
        probs.append(some)
        values.append((some - onehot) / total_rows)
    probs, values = jnp.concatenate(probs, axis=1), jnp.concatenate(values, axis=1)

    def backward(values, scalar, during):
        sums = [None] * len(plan.chunks)

        def multiply(group):
            a, n = plan.pair_range(group)
            sides = back(plan, where, group, order.after(values[a : a + n]), high, low)
            for c, side in zip(plan.pairs[group], sides):
                sums[c] = ClipSum(plan, side, plan.turns[c])
            order.note(sides[-1][0])

        def go(*chunks):
            for c in chunks:
                if not sums[c].done():
                    sums[c].advance(order)

        multiply(0)
        if scalar is not None:
            scalar.advance(order)
        go(0)
        multiply(1)
        if scalar is not None:
            scalar.advance(order)
        go(0, 1, 2)
        multiply(2)
        if scalar is not None:
            scalar.advance(order)
        go(0, 2, 1, 3)
        result = during(scalar.result(order)) if scalar is not None else None
        go(0, 2, 1, 3, 2, 1, 0, 3)
        return sums, go, result

    def forward(sums, go, step=None, direction=None):
        vectors, found = None, []

        def multiply(group):
            pieces = [sums[c].pieces(order) for c in plan.pairs[group]]
            out, halves = forth(plan, where, group, pieces, high, low, vectors, step, direction)
            order.note(halves[0][0])
            found.append(FeatSum(plan, halves[0], bit, 1))
            return out

        vectors = multiply(0)
        go(3, 2, 1)
        vectors = multiply(1)
        found[0].advance(order)
        go(3)
        vectors = multiply(2)
        found[0].advance(order)
        found[1].advance(order)
        found[2].advance(order)
        found[1].advance(order)
        found[2].advance(order)
        tangents = [f.result(order) for f in found]
        inner = sum(t[-ROWS8 : 2 - ROWS8, 0] for t in tangents)
        return vectors, jnp.concatenate([t[:-ROWS8] for t in tangents], axis=0), inner

    def bend(tangent):
        weighted = probs * tangent
        bent = (weighted - probs * jnp.sum(weighted, axis=0, keepdims=True)) / total_rows
        order.note(bent)
        return bent, ScalarSum(plan, jnp.sum(bent * tangent))

    sums, go, _ = backward(values, None, None)
    direction, tangent, inner = forward(sums, go)
    norm0 = inner[0]
    bent, curvature = bend(tangent)

    sums, go, step0 = backward(bent, curvature, lambda total: norm0 / (total + damping * norm0))
    residual, fresh, inner = forward(sums, go, step0, direction)
    norm1, cross = inner[0], inner[1]
    ratio = norm1 / norm0
    bent, curvature = bend(fresh + ratio * tangent)
    length = norm1 + 2.0 * ratio * cross + ratio * ratio * norm0

    sums, go, step1 = backward(bent, curvature, lambda total: norm1 / (total + damping * length))
    moved = order.after(weights) + (step0 + step1 * ratio) * direction + step1 * residual
    order.note(moved)
    go(3, 2, 1)
    scalars, out = jnp.stack([step1, ratio]), None
    for group, members in enumerate(plan.pairs):
        pieces = [sums[c].pieces(order) for c in members]
        if group == 1:
            go(3)
        out = last(plan, where, group, scalars, pieces, direction, residual, out)
        order.note(out)
    return moved, out


def solution(mesh):
    in_specs = (P("clip", "feat"), P(None, "feat"), P("clip"))
    out_specs = (P(None, "feat"), P(None, "feat"))
    return jax.shard_map(local, mesh=mesh, in_specs=in_specs, out_specs=out_specs, check_vma=False)
```

```python
import functools

import jax
import jax.numpy as jnp
from jax import lax
from jax.experimental import pallas as pl
from jax.experimental.pallas import tpu as pltpu
from jax.sharding import PartitionSpec as P

damping = 0.01
F32, BF16 = jnp.float32, jnp.bfloat16
LANES, ROWS8, UNIT = 128, 8, 16
NT = (((1,), (1,)), ((), ()))
NN = (((1,), (0,)), ((), ()))
VMEM_LIMIT = 52 * 1024 * 1024


def parts_of(x):
    high = x.astype(BF16)
    return high, (x - high.astype(F32)).astype(BF16)


def dot3(x, high, low, dims):
    x_high, x_low = parts_of(x)
    dot = functools.partial(lax.dot_general, dimension_numbers=dims, preferred_element_type=F32)
    return dot(x_high, high) + (dot(x_low, high) + dot(x_high, low))


def params():
    return pltpu.CompilerParams(vmem_limit_bytes=VMEM_LIMIT)


class Plan:
    def __init__(self, rows, feats, classes, n_clip, n_feat):
        self.rows, self.feats, self.classes = rows, feats, classes
        self.n_clip, self.n_feat = n_clip, n_feat
        units = classes // UNIT
        small = units // 5
        middle = (units - 2 * small) // 2
        sizes = [UNIT * k for k in (units - 2 * small - middle, middle, small, small)]
        starts = [sum(sizes[:k]) for k in range(4)]
        self.chunks = list(zip(starts, sizes))
        self.pairs = [(0, 1), (2, 3)]
        self.turns = [(0, 1), (1, 0), (0, 1), (1, 0)]
        strides = [1 << k for k in range(1, n_clip.bit_length() - 1)]
        self.levels, block = [], feats
        while strides and block % (2 * LANES) == 0:
            self.levels.append(strides.pop(0))
            block //= 2
        self.doubled = strides
        self.block, self.nb = block, feats // block
        self.rows_step = next(n for n in (256, 128, rows) if rows % n == 0)

    def pair_range(self, pair):
        first, last = self.pairs[pair][0], self.pairs[pair][-1]
        start = self.chunks[first][0]
        return start, self.chunks[last][0] + self.chunks[last][1] - start


def swap(x, axis, stride):
    size = lax.axis_size(axis)
    return lax.ppermute(x, axis, [(i, i ^ stride) for i in range(size)])


def first_body(plan, s_ref, f_ref, w_ref, *rest):
    high_ref, low_ref, send_ref, keep_ref, acc = rest[-5:]
    p = pl.program_id(0)
    high, low = parts_of(f_ref[...])
    high_ref[...] = high
    low_ref[...] = low
    part = dot3(w_ref[...], high, low, NT)

    @pl.when(p == 0)
    def _():
        acc[...] = part

    @pl.when(p > 0)
    def _():
        acc[...] += part

    @pl.when(p == plan.nb - 1)
    def _():
        half = plan.classes // 2
        bit = s_ref[2]
        send_ref[...] = acc[pl.ds(pl.multiple_of((1 - bit) * half, ROWS8), half), :]
        keep_ref[...] = acc[pl.ds(pl.multiple_of(bit * half, ROWS8), half), :]


def first(plan, where, features, weights, part, split):
    rows, block, step = plan.rows, plan.block, plan.rows_step
    half = plan.classes // 2
    operands = [features, weights]
    in_specs = [
        pl.BlockSpec((step, block), lambda p, s: (part, p ^ s[0])),
        pl.BlockSpec((plan.classes, block), lambda p, s: (0, p ^ s[0])),
    ]
    aliases = {}
    if split is not None:
        aliases = {3: 0, 4: 1}
        operands += list(split)
        in_specs += [pl.BlockSpec(memory_space=pl.ANY)] * 2
    high, low, send, keep = pl.pallas_call(
        functools.partial(first_body, plan),
        out_shape=[jax.ShapeDtypeStruct((rows, plan.feats), BF16)] * 2
        + [jax.ShapeDtypeStruct((half, step), F32)] * 2,
        grid_spec=pltpu.PrefetchScalarGridSpec(
            num_scalar_prefetch=1,
            grid=(plan.nb,),
            in_specs=in_specs,
            out_specs=[pl.BlockSpec((step, block), lambda p, s: (part, p))] * 2
            + [pl.BlockSpec((half, step), lambda p, s: (0, 0))] * 2,
            scratch_shapes=[pltpu.VMEM((plan.classes, step), F32)],
        ),
        input_output_aliases=aliases,
        compiler_params=params(),
        cost_estimate=pl.CostEstimate(
            flops=6 * plan.classes * step * plan.feats,
            bytes_accessed=4 * plan.feats * (2 * step + plan.classes),
            transcendentals=0,
        ),
        name="split_and_logits",
    )(where, *operands)
    return (high, low), (send, keep)


def back_body(plan, s_ref, g_ref, high_ref, low_ref, *outs):
    core = s_ref[1]
    some, ends = [], []
    for a, n in plan.chunks:
        h = n // 2
        for side in (core, 1 - core):
            some.append(g_ref[pl.ds(pl.multiple_of(a + side * h, ROWS8), h), :])
            ends.append((ends[-1] if ends else 0) + h)
    x = jnp.concatenate(some, axis=0)
    width = 2 * LANES
    for k in range(0, plan.block, width):
        w = min(width, plan.block - k)
        part = dot3(x, high_ref[:, k : k + w], low_ref[:, k : k + w], NN)
        for out, start, end in zip(outs, [0] + ends, ends):
            out[:, k : k + w] = part[start:end]


def back(plan, where, values, high, low):
    rows, block, feats, classes = plan.rows, plan.block, plan.feats, plan.classes
    outs, specs = [], []
    for _, n in plan.chunks:
        outs += [jax.ShapeDtypeStruct((n // 2, feats), F32)] * 2
        specs += [pl.BlockSpec((n // 2, block), lambda p, s: (0, p))] * 2
    result = pl.pallas_call(
        functools.partial(back_body, plan),
        out_shape=outs,
        grid_spec=pltpu.PrefetchScalarGridSpec(
            num_scalar_prefetch=1,
            grid=(plan.nb,),
            in_specs=[
                pl.BlockSpec((classes, rows), lambda p, s: (0, 0)),
                pl.BlockSpec((rows, block), lambda p, s: (0, p)),
                pl.BlockSpec((rows, block), lambda p, s: (0, p)),
            ],
            out_specs=specs,
        ),
        compiler_params=params(),
        cost_estimate=pl.CostEstimate(
            flops=6 * classes * rows * feats, bytes_accessed=4 * feats * (rows + classes), transcendentals=0
        ),
        name="back_all",
    )(where, values, high, low)
    return [tuple(result[2 * k : 2 * k + 2]) for k in range(len(plan.chunks))]


class Pieces:
    def __init__(self, places, mine, theirs):
        self.places = (places, [tuple(p for place in places for p in place)])
        self.mine, self.theirs = mine, theirs

    def flat(self):
        return list(self.mine) + [self.theirs]


def gather_rows(plan, pair, chunks, s_ref, refs, position, target):
    core = s_ref[1]
    base = plan.pair_range(pair)[0]
    refs = list(refs)
    for c, places in zip(plan.pairs[pair], chunks):
        a, n = plan.chunks[c]
        h = n // 2
        for side, some in zip((core, 1 - core), places):
            for place in some:
                ref = refs.pop(0)
                if position in place:
                    k = place.index(position) * plan.block
                    target[pl.ds(pl.multiple_of(a - base + side * h, ROWS8), h), :] = ref[:, k : k + plan.block]


def forth_body(plan, pair, step, chunks, s_ref, *refs):
    nb = plan.nb
    refs = list(refs)
    scalar_ref = refs.pop(0) if step else None
    n_pieces = sum(len(some) for places in chunks for some in places)
    pieces, refs = refs[:n_pieces], refs[n_pieces:]
    direction_ref = refs.pop(0) if step else None
    high_ref, low_ref = refs[:2]
    n_ranges = len(tangent_ranges(plan, pair))
    target, acc, sums = refs[-3:]
    vector_ref, outs = refs[-4 - 2 * n_ranges], refs[-3 - 2 * n_ranges : -3]
    n_pair = plan.pair_range(pair)[1]
    p = pl.program_id(0)
    for position in range(nb):

        @pl.when(p == position)
        def _():
            gather_rows(plan, pair, chunks, s_ref, pieces, position, target)

    if step:
        direction = direction_ref[...]
        vector = direction - scalar_ref[0] * (target[...] + damping * direction)
    else:
        vector = -target[...]
    vector_ref[...] = vector
    part = dot3(vector, high_ref[...], low_ref[...], NT)
    square = jnp.sum(vector * vector).reshape(1, 1)
    cross = jnp.sum(vector * direction).reshape(1, 1) if step else square
    ids = lax.broadcasted_iota(jnp.int32, (ROWS8, plan.rows), 0)
    new = jnp.where(ids == 0, square, jnp.where(ids == 1, cross, 0.0))

    @pl.when(p == 0)
    def _():
        acc[:n_pair, :] = part
        sums[...] = new

    @pl.when(p > 0)
    def _():
        acc[:n_pair, :] += part
        sums[...] += new

    @pl.when(p == nb - 1)
    def _():
        acc[n_pair:, :] = sums[...]
        half = plan.rows // 2
        bit = s_ref[2]
        keep = pl.multiple_of(bit * half, LANES)
        send = pl.multiple_of((1 - bit) * half, LANES)
        for k, (a, n) in enumerate(tangent_ranges(plan, pair)):
            outs[2 * k][...] = acc[a : a + n, pl.ds(send, half)]
            outs[2 * k + 1][...] = acc[a : a + n, pl.ds(keep, half)]


def tangent_ranges(plan, pair):
    return [(0, plan.pair_range(pair)[1] + ROWS8)]


def placed(plan, pair):
    base, n_pair = plan.pair_range(pair)
    return pl.BlockSpec(
        (pl.Element(n_pair), pl.Element(plan.block)), lambda p, s: (base, (p ^ s[0]) * plan.block)
    )


def forth(plan, where, pair, pieces, high, low, vectors, step=None, direction=None):
    rows, block, feats, nb = plan.rows, plan.block, plan.feats, plan.nb
    half = rows // 2
    n_pair = plan.pair_range(pair)[1]
    operands, in_specs = [], []
    if step is not None:
        operands.append(step.reshape(1))
        in_specs.append(pl.BlockSpec(memory_space=pltpu.SMEM))
    for piece in pieces:
        for x in piece.flat():
            operands.append(x)
            in_specs.append(pl.BlockSpec(x.shape, lambda p, s: (0, 0)))
    if step is not None:
        operands.append(direction)
        in_specs.append(placed(plan, pair))
    operands += [high, low]
    in_specs += [pl.BlockSpec((rows, block), lambda p, s: (0, p))] * 2
    aliases = {}
    if vectors is not None:
        aliases = {len(operands) + 1: 0}
        operands.append(vectors)
        in_specs.append(pl.BlockSpec(memory_space=pl.ANY))
    outs, specs = [jax.ShapeDtypeStruct((plan.classes, feats), F32)], [placed(plan, pair)]
    for _, n in tangent_ranges(plan, pair):
        outs += [jax.ShapeDtypeStruct((n, half), F32)] * 2
        specs += [pl.BlockSpec((n, half), lambda p, s: (0, 0))] * 2
    result = pl.pallas_call(
        functools.partial(forth_body, plan, pair, step is not None, [piece.places for piece in pieces]),
        out_shape=outs,
        grid_spec=pltpu.PrefetchScalarGridSpec(
            num_scalar_prefetch=1,
            grid=(nb,),
            in_specs=in_specs,
            out_specs=specs,
            scratch_shapes=[
                pltpu.VMEM((n_pair, block), F32),
                pltpu.VMEM((n_pair + ROWS8, rows), F32),
                pltpu.VMEM((ROWS8, rows), F32),
            ],
        ),
        input_output_aliases=aliases,
        compiler_params=params(),
        cost_estimate=pl.CostEstimate(
            flops=6 * n_pair * rows * feats, bytes_accessed=4 * feats * (rows + 3 * n_pair), transcendentals=0
        ),
        name="forth_pair",
    )(where, *operands)
    return result[0], [tuple(result[1 + 2 * k : 3 + 2 * k]) for k in range(len(tangent_ranges(plan, pair)))]


def last_body(plan, pair, chunks, s_ref, scalar_ref, *refs):
    nb = plan.nb
    refs = list(refs)
    n_pieces = sum(len(some) for places in chunks for some in places)
    pieces = refs[:n_pieces]
    direction_ref, residual_ref = refs[n_pieces : n_pieces + 2]
    out_ref, target, along, ready, arrived, left = refs[-6:]
    base, n_pair = plan.pair_range(pair)

    def place(ref, position):
        column = pl.multiple_of((position ^ s_ref[0]) * plan.block, LANES)
        return ref.at[pl.ds(base, n_pair), pl.ds(column, plan.block)]

    reads = []
    for q in range(nb):
        reads.append(pltpu.make_async_copy(place(direction_ref, q), along.at[q], arrived.at[0, q]))
        reads.append(pltpu.make_async_copy(place(residual_ref, q), ready.at[q], arrived.at[1, q]))
    writes = [pltpu.make_async_copy(ready.at[q], place(out_ref, q), left.at[q]) for q in range(nb)]
    for read in reads:
        read.start()
    for q in range(nb):
        gather_rows(plan, pair, chunks, s_ref, pieces, q, target)
        reads[2 * q].wait()
        reads[2 * q + 1].wait()
        residual = ready[q]
        following = residual + scalar_ref[1] * along[q]
        ready[q] = residual - scalar_ref[0] * (target[...] + damping * following)
        writes[q].start()
    for write in writes:
        write.wait()


def last(plan, where, pair, scalars, pieces, direction, residual, out):
    block, nb = plan.block, plan.nb
    n_pair = plan.pair_range(pair)[1]
    operands, in_specs = [where, scalars], [pl.BlockSpec(memory_space=pltpu.SMEM)] * 2
    for piece in pieces:
        for x in piece.flat():
            operands.append(x)
            in_specs.append(pl.BlockSpec(memory_space=pltpu.VMEM))
    operands += [direction, residual]
    aliases = {}
    if out is not None:
        aliases = {len(operands): 0}
        operands.append(out)
    in_specs += [pl.BlockSpec(memory_space=pl.ANY)] * (len(operands) - len(in_specs))
    return pl.pallas_call(
        functools.partial(last_body, plan, pair, [piece.places for piece in pieces]),
        out_shape=jax.ShapeDtypeStruct((plan.classes, plan.feats), F32),
        in_specs=in_specs,
        out_specs=pl.BlockSpec(memory_space=pl.ANY),
        scratch_shapes=[
            pltpu.VMEM((n_pair, block), F32),
            pltpu.VMEM((nb, n_pair, block), F32),
            pltpu.VMEM((nb, n_pair, block), F32),
            pltpu.SemaphoreType.DMA((2, nb)),
            pltpu.SemaphoreType.DMA((nb,)),
        ],
        input_output_aliases=aliases,
        compiler_params=params(),
        cost_estimate=pl.CostEstimate(
            flops=6 * n_pair * plan.feats, bytes_accessed=16 * n_pair * plan.feats, transcendentals=0
        ),
        name="last_rows",
    )(*operands)


class Order:
    def __init__(self):
        self.token = None

    def after(self, x):
        if self.token is None:
            return x
        return lax.optimization_barrier((x, self.token))[0]

    def note(self, x):
        self.token = x


def columns(plan, x, positions):
    if list(positions) == list(range(positions[0], positions[-1] + 1)):
        return x[:, positions[0] * plan.block : (positions[-1] + 1) * plan.block]
    return jnp.concatenate([x[:, p * plan.block : (p + 1) * plan.block] for p in positions], axis=1)


class ClipSum:
    def __init__(self, plan, sides, turns):
        self.plan = plan
        self.own, other = sides
        levels = [(stride, 1 << k) for k, stride in enumerate(plan.levels)]
        down, up = (levels[::-1] if turn else levels for turn in turns)
        self.active = list(range(plan.nb))
        self.places, self.mine = [], []
        self.steps = [("core", 1, 0)]
        self.steps += [("scatter", stride, bit) for stride, bit in down]
        self.steps += [("double", stride, 0) for stride in plan.doubled]
        self.steps += [("gather", stride, bit) for stride, bit in up]
        self.kept = self.own
        self.pending = swap(other, "clip", 1)

    def done(self):
        return not self.steps

    def advance(self, order):
        kind, _, bit = self.steps.pop(0)
        got = order.after(self.pending)
        if kind == "gather":
            self.mine.append(got)
            self.places.append(tuple(p | bit for place in self.places for p in place))
        else:
            self.own = self.kept + got
            if not self.steps or self.steps[0][0] == "gather":
                self.places, self.mine = [tuple(self.active)], [self.own]
        kind, stride, bit = self.steps[0] if self.steps else ("core", 1, 0)
        if kind == "scatter":
            rest = [p for p in self.active if not p & bit]
            sent = columns(self.plan, self.own, [self.active.index(p | bit) for p in rest])
            self.kept = columns(self.plan, self.own, [self.active.index(p) for p in rest])
            self.active = rest
        elif kind == "double":
            sent = self.kept = self.own
        else:
            sent = self.mine[0] if len(self.mine) == 1 else jnp.concatenate(self.mine, axis=1)
        order.note(sent)
        self.pending = swap(sent, "clip", stride)

    def pieces(self, order):
        while not self.done():
            self.advance(order)
        return Pieces(self.places, self.mine, order.after(self.pending))


class FeatSum:
    def __init__(self, plan, halves, bit, axis):
        send, self.kept = halves
        self.bit, self.axis = bit, axis
        strides = [1 << k for k in range(plan.n_feat.bit_length() - 1)]
        self.strides = strides + [1]
        self.pending = swap(send, "feat", 1)

    def advance(self, order):
        self.strides.pop(0)
        got = order.after(self.pending)
        if self.strides:
            self.kept = self.kept + got
            self.pending = swap(self.kept, "feat", self.strides[0])
            order.note(self.kept)
        else:
            self.got = got
            order.note(got)

    def result(self, order):
        while self.strides:
            self.advance(order)
        one, two = [self.got, self.kept], [self.kept, self.got]
        return jnp.where(self.bit, jnp.concatenate(one, self.axis), jnp.concatenate(two, self.axis))


class ScalarSum:
    def __init__(self, plan, value):
        self.strides = [1 << k for k in range(plan.n_clip.bit_length() - 1)]
        self.row = jnp.broadcast_to(value, (ROWS8, LANES))
        self.pending = swap(self.row, "clip", 1)

    def advance(self, order):
        if not self.strides:
            return
        self.strides.pop(0)
        self.row = self.row + order.after(self.pending)
        order.note(self.row)
        if self.strides:
            self.pending = swap(self.row, "clip", self.strides[0])

    def result(self, order):
        while self.strides:
            self.advance(order)
        return self.row[0, 0]


def local(features, weights, labels):
    rows, feats = features.shape
    classes = weights.shape[0]
    plan = Plan(rows, feats, classes, lax.axis_size("clip"), lax.axis_size("feat"))
    total_rows = rows * plan.n_clip
    me, bit = lax.axis_index("clip"), lax.axis_index("feat") & 1
    mask = sum(((me // stride) & 1) << k for k, stride in enumerate(plan.levels))
    where = jnp.stack([jnp.asarray(mask), me & 1, bit]).astype(jnp.int32)
    order = Order()
    groups = range(len(plan.pairs))

    split, parts = None, []
    for part in range(rows // plan.rows_step):
        if part > 1:
            parts[part - 2].advance(order)
        split, halves = first(plan, where, order.after(features), weights, part, split)
        order.note(halves[0])
        parts.append(FeatSum(plan, halves, bit, 0))
    for part in range(len(parts) - 1, len(parts) - 3, -1):
        if part > 0:
            parts[part - 1].advance(order)
    high, low = split
    probs, values = [], []
    for part, summed in enumerate(parts):
        logits = summed.result(order)
        top = jnp.max(logits, axis=0, keepdims=True)
        powers = jnp.exp(logits - top)
        some = powers / jnp.sum(powers, axis=0, keepdims=True)
        mine = labels[part * plan.rows_step : (part + 1) * plan.rows_step]
        onehot = (mine[None, :] == jnp.arange(classes, dtype=jnp.int32)[:, None]).astype(F32)
        probs.append(some)
        values.append((some - onehot) / total_rows)
    probs, values = jnp.concatenate(probs, axis=1), jnp.concatenate(values, axis=1)

    def backward(values, scalar=None, during=None, under=None):
        sides = back(plan, where, order.after(values), high, low)
        sums = [ClipSum(plan, side, plan.turns[c]) for c, side in enumerate(sides)]
        order.note(sides[-1][0])
        result = None

        def go(*chunks):
            for c in chunks:
                if not sums[c].done():
                    sums[c].advance(order)

        if scalar is not None:
            scalar.advance(order)
        go(0, 1)
        if scalar is not None:
            scalar.advance(order)
        go(0, 1, 2, 3)
        if scalar is not None:
            result = during(scalar.result(order))
        go(0, 1, 0, 1, 2, 3)
        if under is not None:
            result = under(result)
        go(2, 3, 0, 1, 2, 3)
        return sums, go, result

    def forward(sums, go, step=None, direction=None):
        vectors, found = None, []

        def multiply(group):
            pieces = [sums[c].pieces(order) for c in plan.pairs[group]]
            out, halves = forth(plan, where, group, pieces, high, low, vectors, step, direction)
            order.note(halves[0][0])
            found.append(FeatSum(plan, halves[0], bit, 1))
            return out

        vectors = multiply(0)
        go(2, 3)
        found[0].advance(order)
        vectors = multiply(1)
        found[0].advance(order)
        found[1].advance(order)
        found[0].advance(order)
        tangents = [f.result(order) for f in found]
        inner = sum(t[-ROWS8 : 2 - ROWS8, 0] for t in tangents)
        return vectors, jnp.concatenate([t[:-ROWS8] for t in tangents], axis=0), inner

    def bend(tangent):
        weighted = probs * tangent
        bent = (weighted - probs * jnp.sum(weighted, axis=0, keepdims=True)) / total_rows
        order.note(bent)
        return bent, ScalarSum(plan, jnp.sum(bent * tangent))

    sums, go, _ = backward(values)
    direction, tangent, inner = forward(sums, go)
    norm0 = inner[0]
    bent, curvature = bend(tangent)

    sums, go, step0 = backward(bent, curvature, lambda total: norm0 / (total + damping * norm0))
    residual, fresh, inner = forward(sums, go, step0, direction)
    norm1, cross = inner[0], inner[1]
    ratio = norm1 / norm0
    bent, curvature = bend(fresh + ratio * tangent)
    length = norm1 + 2.0 * ratio * cross + ratio * ratio * norm0

    def under(step1):
        moved = order.after(weights) + (step0 + step1 * ratio) * direction + step1 * residual
        order.note(moved)
        return step1, moved

    sums, go, (step1, moved) = backward(
        bent, curvature, lambda total: norm1 / (total + damping * length), under
    )
    scalars, out = jnp.stack([step1, ratio]), None
    for group, members in enumerate(plan.pairs):
        pieces = [sums[c].pieces(order) for c in members]
        if group == 0:
            go(2, 3)
        out = last(plan, where, group, scalars, pieces, direction, residual, out)
        order.note(out)
    return moved, out


def solution(mesh):
    in_specs = (P("clip", "feat"), P(None, "feat"), P("clip"))
    out_specs = (P(None, "feat"), P(None, "feat"))
    return jax.shard_map(local, mesh=mesh, in_specs=in_specs, out_specs=out_specs, check_vma=False)
```

```python
import functools

import jax
import jax.numpy as jnp
from jax import lax
from jax.experimental import pallas as pl
from jax.experimental.pallas import tpu as pltpu
from jax.sharding import PartitionSpec as P

damping = 0.01
F32, BF16 = jnp.float32, jnp.bfloat16
LANES, ROWS8, UNIT = 128, 8, 16
NT = (((1,), (1,)), ((), ()))
NN = (((1,), (0,)), ((), ()))
VMEM_LIMIT = 32 * 1024 * 1024


def parts_of(x):
    high = x.astype(BF16)
    return high, (x - high.astype(F32)).astype(BF16)


def dot3(x, high, low, dims):
    x_high, x_low = parts_of(x)
    dot = functools.partial(lax.dot_general, dimension_numbers=dims, preferred_element_type=F32)
    return dot(x_high, high) + (dot(x_low, high) + dot(x_high, low))


def params():
    return pltpu.CompilerParams(vmem_limit_bytes=VMEM_LIMIT)


class Plan:
    def __init__(self, rows, feats, classes, n_clip, n_feat):
        self.rows, self.feats, self.classes = rows, feats, classes
        self.n_clip, self.n_feat = n_clip, n_feat
        units = classes // UNIT
        small = units // 5
        middle = (units - 2 * small) // 2
        sizes = [UNIT * k for k in (units - 2 * small - middle, middle, small, small)]
        starts = [sum(sizes[:k]) for k in range(4)]
        self.chunks = list(zip(starts, sizes))
        self.pairs = [(0, 1), (2, 3)]
        self.turns = [(0, 1), (1, 0), (0, 1), (1, 0)]
        strides = [1 << k for k in range(1, n_clip.bit_length() - 1)]
        self.levels, block = [], feats
        while strides and block % (2 * LANES) == 0:
            self.levels.append(strides.pop(0))
            block //= 2
        self.doubled = strides
        self.block, self.nb = block, feats // block
        self.rows_step = next(n for n in (256, 128, rows) if rows % n == 0)

    def pair_range(self, pair):
        first, last = self.pairs[pair][0], self.pairs[pair][-1]
        start = self.chunks[first][0]
        return start, self.chunks[last][0] + self.chunks[last][1] - start


def swap(x, axis, stride):
    size = lax.axis_size(axis)
    return lax.ppermute(x, axis, [(i, i ^ stride) for i in range(size)])


def first_body(plan, s_ref, f_ref, w_ref, *rest):
    high_ref, low_ref, send_ref, keep_ref, acc = rest[-5:]
    p = pl.program_id(0)
    high, low = parts_of(f_ref[...])
    high_ref[...] = high
    low_ref[...] = low
    part = dot3(w_ref[...], high, low, NT)

    @pl.when(p == 0)
    def _():
        acc[...] = part

    @pl.when(p > 0)
    def _():
        acc[...] += part

    @pl.when(p == plan.nb - 1)
    def _():
        half = plan.classes // 2
        bit = s_ref[2]
        send_ref[...] = acc[pl.ds(pl.multiple_of((1 - bit) * half, ROWS8), half), :]
        keep_ref[...] = acc[pl.ds(pl.multiple_of(bit * half, ROWS8), half), :]


def first(plan, where, features, weights, part, split):
    rows, block, step = plan.rows, plan.block, plan.rows_step
    half = plan.classes // 2
    operands = [features, weights]
    in_specs = [
        pl.BlockSpec((step, block), lambda p, s: (part, p ^ s[0])),
        pl.BlockSpec((plan.classes, block), lambda p, s: (0, p ^ s[0])),
    ]
    aliases = {}
    if split is not None:
        aliases = {3: 0, 4: 1}
        operands += list(split)
        in_specs += [pl.BlockSpec(memory_space=pl.ANY)] * 2
    high, low, send, keep = pl.pallas_call(
        functools.partial(first_body, plan),
        out_shape=[jax.ShapeDtypeStruct((rows, plan.feats), BF16)] * 2
        + [jax.ShapeDtypeStruct((half, step), F32)] * 2,
        grid_spec=pltpu.PrefetchScalarGridSpec(
            num_scalar_prefetch=1,
            grid=(plan.nb,),
            in_specs=in_specs,
            out_specs=[pl.BlockSpec((step, block), lambda p, s: (part, p))] * 2
            + [pl.BlockSpec((half, step), lambda p, s: (0, 0))] * 2,
            scratch_shapes=[pltpu.VMEM((plan.classes, step), F32)],
        ),
        input_output_aliases=aliases,
        compiler_params=params(),
        cost_estimate=pl.CostEstimate(
            flops=6 * plan.classes * step * plan.feats,
            bytes_accessed=4 * plan.feats * (2 * step + plan.classes),
            transcendentals=0,
        ),
        name="split_and_logits",
    )(where, *operands)
    return (high, low), (send, keep)


def back_body(plan, group, s_ref, g_ref, high_ref, low_ref, *outs):
    core = s_ref[1]
    base = plan.pair_range(group)[0]
    some, ends = [], []
    for c in plan.pairs[group]:
        a, n = plan.chunks[c]
        h = n // 2
        for side in (core, 1 - core):
            some.append(g_ref[pl.ds(pl.multiple_of(a - base + side * h, ROWS8), h), :])
            ends.append((ends[-1] if ends else 0) + h)
    x = jnp.concatenate(some, axis=0)
    width = 2 * LANES
    for k in range(0, plan.block, width):
        w = min(width, plan.block - k)
        part = dot3(x, high_ref[:, k : k + w], low_ref[:, k : k + w], NN)
        for out, start, end in zip(outs, [0] + ends, ends):
            out[:, k : k + w] = part[start:end]


def back(plan, where, group, values, high, low):
    rows, block, feats = plan.rows, plan.block, plan.feats
    n_group = plan.pair_range(group)[1]
    outs, specs = [], []
    for c in plan.pairs[group]:
        h = plan.chunks[c][1] // 2
        outs += [jax.ShapeDtypeStruct((h, feats), F32)] * 2
        specs += [pl.BlockSpec((h, block), lambda p, s: (0, p))] * 2
    result = pl.pallas_call(
        functools.partial(back_body, plan, group),
        out_shape=outs,
        grid_spec=pltpu.PrefetchScalarGridSpec(
            num_scalar_prefetch=1,
            grid=(plan.nb,),
            in_specs=[
                pl.BlockSpec((n_group, rows), lambda p, s: (0, 0), pipeline_mode=pl.Buffered(1)),
                pl.BlockSpec((rows, block), lambda p, s: (0, p)),
                pl.BlockSpec((rows, block), lambda p, s: (0, p)),
            ],
            out_specs=specs,
        ),
        compiler_params=params(),
        cost_estimate=pl.CostEstimate(
            flops=6 * n_group * rows * feats, bytes_accessed=4 * feats * (rows + n_group), transcendentals=0
        ),
        name="back_group",
    )(where, values, high, low)
    return [tuple(result[2 * k : 2 * k + 2]) for k in range(len(plan.pairs[group]))]


class Pieces:
    def __init__(self, places, mine, theirs):
        self.places = (places, [tuple(p for place in places for p in place)])
        self.mine, self.theirs = mine, theirs

    def flat(self):
        return list(self.mine) + [self.theirs]


def gather_rows(plan, pair, chunks, s_ref, refs, position, target):
    core = s_ref[1]
    base = plan.pair_range(pair)[0]
    refs = list(refs)
    for c, places in zip(plan.pairs[pair], chunks):
        a, n = plan.chunks[c]
        h = n // 2
        for side, some in zip((core, 1 - core), places):
            for place in some:
                ref = refs.pop(0)
                if position in place:
                    k = place.index(position) * plan.block
                    target[pl.ds(pl.multiple_of(a - base + side * h, ROWS8), h), :] = ref[:, k : k + plan.block]


def forth_body(plan, pair, step, chunks, s_ref, *refs):
    nb = plan.nb
    refs = list(refs)
    scalar_ref = refs.pop(0) if step else None
    n_pieces = sum(len(some) for places in chunks for some in places)
    pieces, refs = refs[:n_pieces], refs[n_pieces:]
    direction_ref = refs.pop(0) if step else None
    high_ref, low_ref = refs[:2]
    n_ranges = len(tangent_ranges(plan, pair))
    target, acc, sums = refs[-3:]
    vector_ref, outs = refs[-4 - 2 * n_ranges], refs[-3 - 2 * n_ranges : -3]
    n_pair = plan.pair_range(pair)[1]
    p = pl.program_id(0)
    for position in range(nb):

        @pl.when(p == position)
        def _():
            gather_rows(plan, pair, chunks, s_ref, pieces, position, target)

    if step:
        direction = direction_ref[...]
        vector = direction - scalar_ref[0] * (target[...] + damping * direction)
    else:
        vector = -target[...]
    vector_ref[...] = vector
    part = dot3(vector, high_ref[...], low_ref[...], NT)
    square = jnp.sum(vector * vector).reshape(1, 1)
    cross = jnp.sum(vector * direction).reshape(1, 1) if step else square
    ids = lax.broadcasted_iota(jnp.int32, (ROWS8, plan.rows), 0)
    new = jnp.where(ids == 0, square, jnp.where(ids == 1, cross, 0.0))

    @pl.when(p == 0)
    def _():
        acc[:n_pair, :] = part
        sums[...] = new

    @pl.when(p > 0)
    def _():
        acc[:n_pair, :] += part
        sums[...] += new

    @pl.when(p == nb - 1)
    def _():
        acc[n_pair:, :] = sums[...]
        half = plan.rows // 2
        bit = s_ref[2]
        keep = pl.multiple_of(bit * half, LANES)
        send = pl.multiple_of((1 - bit) * half, LANES)
        for k, (a, n) in enumerate(tangent_ranges(plan, pair)):
            outs[2 * k][...] = acc[a : a + n, pl.ds(send, half)]
            outs[2 * k + 1][...] = acc[a : a + n, pl.ds(keep, half)]


def tangent_ranges(plan, pair):
    return [(0, plan.pair_range(pair)[1] + ROWS8)]


def placed(plan, pair):
    base, n_pair = plan.pair_range(pair)
    return pl.BlockSpec(
        (pl.Element(n_pair), pl.Element(plan.block)), lambda p, s: (base, (p ^ s[0]) * plan.block)
    )


def forth(plan, where, pair, pieces, high, low, vectors, step=None, direction=None):
    rows, block, feats, nb = plan.rows, plan.block, plan.feats, plan.nb
    half = rows // 2
    n_pair = plan.pair_range(pair)[1]
    operands, in_specs = [], []
    if step is not None:
        operands.append(step.reshape(1))
        in_specs.append(pl.BlockSpec(memory_space=pltpu.SMEM))
    for piece in pieces:
        for x in piece.flat():
            operands.append(x)
            in_specs.append(pl.BlockSpec(x.shape, lambda p, s: (0, 0), pipeline_mode=pl.Buffered(1)))
    if step is not None:
        operands.append(direction)
        in_specs.append(placed(plan, pair))
    operands += [high, low]
    in_specs += [pl.BlockSpec((rows, block), lambda p, s: (0, p))] * 2
    aliases = {}
    if vectors is not None:
        aliases = {len(operands) + 1: 0}
        operands.append(vectors)
        in_specs.append(pl.BlockSpec(memory_space=pl.ANY))
    outs, specs = [jax.ShapeDtypeStruct((plan.classes, feats), F32)], [placed(plan, pair)]
    for _, n in tangent_ranges(plan, pair):
        outs += [jax.ShapeDtypeStruct((n, half), F32)] * 2
        specs += [pl.BlockSpec((n, half), lambda p, s: (0, 0))] * 2
    result = pl.pallas_call(
        functools.partial(forth_body, plan, pair, step is not None, [piece.places for piece in pieces]),
        out_shape=outs,
        grid_spec=pltpu.PrefetchScalarGridSpec(
            num_scalar_prefetch=1,
            grid=(nb,),
            in_specs=in_specs,
            out_specs=specs,
            scratch_shapes=[
                pltpu.VMEM((n_pair, block), F32),
                pltpu.VMEM((n_pair + ROWS8, rows), F32),
                pltpu.VMEM((ROWS8, rows), F32),
            ],
        ),
        input_output_aliases=aliases,
        compiler_params=params(),
        cost_estimate=pl.CostEstimate(
            flops=6 * n_pair * rows * feats, bytes_accessed=4 * feats * (rows + 3 * n_pair), transcendentals=0
        ),
        name="forth_pair",
    )(where, *operands)
    return result[0], [tuple(result[1 + 2 * k : 3 + 2 * k]) for k in range(len(tangent_ranges(plan, pair)))]


def last_body(plan, pair, chunks, s_ref, scalar_ref, *refs):
    nb = plan.nb
    refs = list(refs)
    n_pieces = sum(len(some) for places in chunks for some in places)
    pieces = refs[:n_pieces]
    direction_ref, residual_ref = refs[n_pieces : n_pieces + 2]
    out_ref, target, along, ready, arrived, left = refs[-6:]
    base, n_pair = plan.pair_range(pair)

    def place(ref, position):
        column = pl.multiple_of((position ^ s_ref[0]) * plan.block, LANES)
        return ref.at[pl.ds(base, n_pair), pl.ds(column, plan.block)]

    reads = []
    for q in range(nb):
        reads.append(pltpu.make_async_copy(place(direction_ref, q), along.at[q], arrived.at[0, q]))
        reads.append(pltpu.make_async_copy(place(residual_ref, q), ready.at[q], arrived.at[1, q]))
    writes = [pltpu.make_async_copy(ready.at[q], place(out_ref, q), left.at[q]) for q in range(nb)]
    for read in reads:
        read.start()
    for q in range(nb):
        gather_rows(plan, pair, chunks, s_ref, pieces, q, target)
        reads[2 * q].wait()
        reads[2 * q + 1].wait()
        residual = ready[q]
        following = residual + scalar_ref[1] * along[q]
        ready[q] = residual - scalar_ref[0] * (target[...] + damping * following)
        writes[q].start()
    for write in writes:
        write.wait()


def last(plan, where, pair, scalars, pieces, direction, residual, out):
    block, nb = plan.block, plan.nb
    n_pair = plan.pair_range(pair)[1]
    operands, in_specs = [where, scalars], [pl.BlockSpec(memory_space=pltpu.SMEM)] * 2
    for piece in pieces:
        for x in piece.flat():
            operands.append(x)
            in_specs.append(pl.BlockSpec(memory_space=pltpu.VMEM))
    operands += [direction, residual]
    aliases = {}
    if out is not None:
        aliases = {len(operands): 0}
        operands.append(out)
    in_specs += [pl.BlockSpec(memory_space=pl.ANY)] * (len(operands) - len(in_specs))
    return pl.pallas_call(
        functools.partial(last_body, plan, pair, [piece.places for piece in pieces]),
        out_shape=jax.ShapeDtypeStruct((plan.classes, plan.feats), F32),
        in_specs=in_specs,
        out_specs=pl.BlockSpec(memory_space=pl.ANY),
        scratch_shapes=[
            pltpu.VMEM((n_pair, block), F32),
            pltpu.VMEM((nb, n_pair, block), F32),
            pltpu.VMEM((nb, n_pair, block), F32),
            pltpu.SemaphoreType.DMA((2, nb)),
            pltpu.SemaphoreType.DMA((nb,)),
        ],
        input_output_aliases=aliases,
        compiler_params=params(),
        cost_estimate=pl.CostEstimate(
            flops=6 * n_pair * plan.feats, bytes_accessed=16 * n_pair * plan.feats, transcendentals=0
        ),
        name="last_rows",
    )(*operands)


class Order:
    def __init__(self):
        self.token = None

    def after(self, x):
        if self.token is None:
            return x
        return lax.optimization_barrier((x, self.token))[0]

    def note(self, x):
        self.token = x


def columns(plan, x, positions):
    if list(positions) == list(range(positions[0], positions[-1] + 1)):
        return x[:, positions[0] * plan.block : (positions[-1] + 1) * plan.block]
    return jnp.concatenate([x[:, p * plan.block : (p + 1) * plan.block] for p in positions], axis=1)


class ClipSum:
    def __init__(self, plan, sides, turns):
        self.plan = plan
        self.own, other = sides
        levels = [(stride, 1 << k) for k, stride in enumerate(plan.levels)]
        down, up = (levels[::-1] if turn else levels for turn in turns)
        self.active = list(range(plan.nb))
        self.places, self.mine = [], []
        self.steps = [("core", 1, 0)]
        self.steps += [("scatter", stride, bit) for stride, bit in down]
        self.steps += [("double", stride, 0) for stride in plan.doubled]
        self.steps += [("gather", stride, bit) for stride, bit in up]
        self.kept = self.own
        self.pending = swap(other, "clip", 1)

    def done(self):
        return not self.steps

    def advance(self, order):
        kind, _, bit = self.steps.pop(0)
        got = order.after(self.pending)
        if kind == "gather":
            self.mine.append(got)
            self.places.append(tuple(p | bit for place in self.places for p in place))
        else:
            self.own = self.kept + got
            if not self.steps or self.steps[0][0] == "gather":
                self.places, self.mine = [tuple(self.active)], [self.own]
        kind, stride, bit = self.steps[0] if self.steps else ("core", 1, 0)
        if kind == "scatter":
            rest = [p for p in self.active if not p & bit]
            sent = columns(self.plan, self.own, [self.active.index(p | bit) for p in rest])
            self.kept = columns(self.plan, self.own, [self.active.index(p) for p in rest])
            self.active = rest
        elif kind == "double":
            sent = self.kept = self.own
        else:
            sent = self.mine[0] if len(self.mine) == 1 else jnp.concatenate(self.mine, axis=1)
        order.note(sent)
        self.pending = swap(sent, "clip", stride)

    def pieces(self, order):
        while not self.done():
            self.advance(order)
        return Pieces(self.places, self.mine, order.after(self.pending))


class FeatSum:
    def __init__(self, plan, halves, bit, axis):
        send, self.kept = halves
        self.bit, self.axis = bit, axis
        strides = [1 << k for k in range(plan.n_feat.bit_length() - 1)]
        self.strides = strides + [1]
        self.pending = swap(send, "feat", 1)

    def advance(self, order):
        self.strides.pop(0)
        got = order.after(self.pending)
        if self.strides:
            self.kept = self.kept + got
            self.pending = swap(self.kept, "feat", self.strides[0])
            order.note(self.kept)
        else:
            self.got = got
            order.note(got)

    def result(self, order):
        while self.strides:
            self.advance(order)
        one, two = [self.got, self.kept], [self.kept, self.got]
        return jnp.where(self.bit, jnp.concatenate(one, self.axis), jnp.concatenate(two, self.axis))


class ScalarSum:
    def __init__(self, plan, value):
        self.strides = [1 << k for k in range(plan.n_clip.bit_length() - 1)]
        self.row = jnp.broadcast_to(value, (ROWS8, LANES))
        self.pending = swap(self.row, "clip", 1)

    def advance(self, order):
        if not self.strides:
            return
        self.strides.pop(0)
        self.row = self.row + order.after(self.pending)
        order.note(self.row)
        if self.strides:
            self.pending = swap(self.row, "clip", self.strides[0])

    def result(self, order):
        while self.strides:
            self.advance(order)
        return self.row[0, 0]


def local(features, weights, labels):
    rows, feats = features.shape
    classes = weights.shape[0]
    plan = Plan(rows, feats, classes, lax.axis_size("clip"), lax.axis_size("feat"))
    total_rows = rows * plan.n_clip
    me, bit = lax.axis_index("clip"), lax.axis_index("feat") & 1
    mask = sum(((me // stride) & 1) << k for k, stride in enumerate(plan.levels))
    where = jnp.stack([jnp.asarray(mask), me & 1, bit]).astype(jnp.int32)
    order = Order()
    groups = range(len(plan.pairs))

    split, parts = None, []
    for part in range(rows // plan.rows_step):
        if part > 1:
            parts[part - 2].advance(order)
        split, halves = first(plan, where, order.after(features), weights, part, split)
        order.note(halves[0])
        parts.append(FeatSum(plan, halves, bit, 0))
    for part in range(len(parts) - 1, len(parts) - 3, -1):
        if part > 0:
            parts[part - 1].advance(order)
    high, low = split
    probs, values = [], []
    for part, summed in enumerate(parts):
        logits = summed.result(order)
        top = jnp.max(logits, axis=0, keepdims=True)
        powers = jnp.exp(logits - top)
        some = powers / jnp.sum(powers, axis=0, keepdims=True)
        mine = labels[part * plan.rows_step : (part + 1) * plan.rows_step]
        onehot = (mine[None, :] == jnp.arange(classes, dtype=jnp.int32)[:, None]).astype(F32)
        probs.append(some)
        values.append((some - onehot) / total_rows)
    probs, values = jnp.concatenate(probs, axis=1), jnp.concatenate(values, axis=1)

    def backward(values, scalar=None, during=None, under=None):
        sums, result = [None] * len(plan.chunks), None

        def multiply(group):
            a, n = plan.pair_range(group)
            sides = back(plan, where, group, order.after(values[a : a + n]), high, low)
            for c, side in zip(plan.pairs[group], sides):
                sums[c] = ClipSum(plan, side, plan.turns[c])
            order.note(sides[-1][0])

        def go(*chunks):
            for c in chunks:
                if not sums[c].done():
                    sums[c].advance(order)

        multiply(0)
        if scalar is not None:
            scalar.advance(order)
        go(0, 1)
        multiply(1)
        if scalar is not None:
            scalar.advance(order)
        go(0, 1, 2, 3)
        if scalar is not None:
            result = during(scalar.result(order))
        if under is not None:
            result = under(result)
        go(0, 1, 2, 3, 0, 1, 2, 3, 2, 3, 0, 1)
        return sums, go, result

    def forward(sums, go, step=None, direction=None):
        vectors, found = None, []

        def multiply(group):
            pieces = [sums[c].pieces(order) for c in plan.pairs[group]]
            out, halves = forth(plan, where, group, pieces, high, low, vectors, step, direction)
            order.note(halves[0][0])
            found.append(FeatSum(plan, halves[0], bit, 1))
            return out

        vectors = multiply(0)
        go(2, 3)
        vectors = multiply(1)
        for k in (0, 1, 0, 1):
            found[k].advance(order)
        tangents = [f.result(order) for f in found]
        inner = sum(t[-ROWS8 : 2 - ROWS8, 0] for t in tangents)
        return vectors, jnp.concatenate([t[:-ROWS8] for t in tangents], axis=0), inner

    def bend(tangent):
        weighted = probs * tangent
        bent = (weighted - probs * jnp.sum(weighted, axis=0, keepdims=True)) / total_rows
        order.note(bent)
        return bent, ScalarSum(plan, jnp.sum(bent * tangent))

    sums, go, _ = backward(values)
    direction, tangent, inner = forward(sums, go)
    norm0 = inner[0]
    bent, curvature = bend(tangent)

    sums, go, step0 = backward(bent, curvature, lambda total: norm0 / (total + damping * norm0))
    residual, fresh, inner = forward(sums, go, step0, direction)
    norm1, cross = inner[0], inner[1]
    ratio = norm1 / norm0
    bent, curvature = bend(fresh + ratio * tangent)
    length = norm1 + 2.0 * ratio * cross + ratio * ratio * norm0

    def under(step1):
        moved = order.after(weights) + (step0 + step1 * ratio) * direction + step1 * residual
        order.note(moved)
        return step1, moved

    sums, go, (step1, moved) = backward(
        bent, curvature, lambda total: norm1 / (total + damping * length), under
    )
    scalars, out = jnp.stack([step1, ratio]), None
    for group, members in enumerate(plan.pairs):
        pieces = [sums[c].pieces(order) for c in members]
        if group == 0:
            go(2, 3)
        out = last(plan, where, group, scalars, pieces, direction, residual, out)
        order.note(out)
    return moved, out


def solution(mesh):
    in_specs = (P("clip", "feat"), P(None, "feat"), P("clip"))
    out_specs = (P(None, "feat"), P(None, "feat"))
    return jax.shard_map(local, mesh=mesh, in_specs=in_specs, out_specs=out_specs, check_vma=False)
```

```python
import functools

import jax
import jax.numpy as jnp
from jax import lax
from jax.experimental import pallas as pl
from jax.experimental.pallas import tpu as pltpu
from jax.sharding import PartitionSpec as P

damping = 0.01
F32, BF16 = jnp.float32, jnp.bfloat16
LANES, ROWS8, UNIT = 128, 8, 16
NT = (((1,), (1,)), ((), ()))
NN = (((1,), (0,)), ((), ()))
MIB = 1024 * 1024


def parts_of(x):
    high = x.astype(BF16)
    return high, (x - high.astype(F32)).astype(BF16)


def dot3(x, high, low, dims):
    x_high, x_low = parts_of(x)
    dot = functools.partial(lax.dot_general, dimension_numbers=dims, preferred_element_type=F32)
    return dot(x_high, high) + (dot(x_low, high) + dot(x_high, low))


def params(mib):
    return pltpu.CompilerParams(vmem_limit_bytes=mib * MIB)


class Plan:
    def __init__(self, rows, feats, classes, n_clip, n_feat):
        self.rows, self.feats, self.classes = rows, feats, classes
        self.n_clip, self.n_feat = n_clip, n_feat
        units = classes // UNIT
        small = units // 5
        middle = (units - 2 * small) // 2
        sizes = [UNIT * k for k in (units - 2 * small - middle, middle, small, small)]
        starts = [sum(sizes[:k]) for k in range(4)]
        self.chunks = list(zip(starts, sizes))
        self.pairs = [(0, 1), (2, 3)]
        self.turns = [(0, 1), (1, 0), (0, 1), (1, 0)]
        strides = [1 << k for k in range(1, n_clip.bit_length() - 1)]
        self.levels, block = [], feats
        while strides and block % (2 * LANES) == 0:
            self.levels.append(strides.pop(0))
            block //= 2
        self.doubled = strides
        self.block, self.nb = block, feats // block
        self.rows_step = next(n for n in (256, 128, rows) if rows % n == 0)

    def pair_range(self, pair):
        first, last = self.pairs[pair][0], self.pairs[pair][-1]
        start = self.chunks[first][0]
        return start, self.chunks[last][0] + self.chunks[last][1] - start


def swap(x, axis, stride):
    size = lax.axis_size(axis)
    return lax.ppermute(x, axis, [(i, i ^ stride) for i in range(size)])


def first_body(plan, s_ref, f_ref, w_ref, *rest):
    high_ref, low_ref, send_ref, keep_ref, acc = rest[-5:]
    p = pl.program_id(0)
    high, low = parts_of(f_ref[...])
    high_ref[...] = high
    low_ref[...] = low
    part = dot3(w_ref[...], high, low, NT)

    @pl.when(p == 0)
    def _():
        acc[...] = part

    @pl.when(p > 0)
    def _():
        acc[...] += part

    @pl.when(p == plan.nb - 1)
    def _():
        half = plan.classes // 2
        bit = s_ref[2]
        send_ref[...] = acc[pl.ds(pl.multiple_of((1 - bit) * half, ROWS8), half), :]
        keep_ref[...] = acc[pl.ds(pl.multiple_of(bit * half, ROWS8), half), :]


def first(plan, where, features, weights, part, split):
    rows, block, step = plan.rows, plan.block, plan.rows_step
    half = plan.classes // 2
    operands = [features, weights]
    in_specs = [
        pl.BlockSpec((step, block), lambda p, s: (part, p ^ s[0])),
        pl.BlockSpec((plan.classes, block), lambda p, s: (0, p ^ s[0])),
    ]
    aliases = {}
    if split is not None:
        aliases = {3: 0, 4: 1}
        operands += list(split)
        in_specs += [pl.BlockSpec(memory_space=pl.ANY)] * 2
    high, low, send, keep = pl.pallas_call(
        functools.partial(first_body, plan),
        out_shape=[jax.ShapeDtypeStruct((rows, plan.feats), BF16)] * 2
        + [jax.ShapeDtypeStruct((half, step), F32)] * 2,
        grid_spec=pltpu.PrefetchScalarGridSpec(
            num_scalar_prefetch=1,
            grid=(plan.nb,),
            in_specs=in_specs,
            out_specs=[pl.BlockSpec((step, block), lambda p, s: (part, p))] * 2
            + [pl.BlockSpec((half, step), lambda p, s: (0, 0))] * 2,
            scratch_shapes=[pltpu.VMEM((plan.classes, step), F32)],
        ),
        input_output_aliases=aliases,
        compiler_params=params(20),
        cost_estimate=pl.CostEstimate(
            flops=6 * plan.classes * step * plan.feats,
            bytes_accessed=4 * plan.feats * (2 * step + plan.classes),
            transcendentals=0,
        ),
        name="split_and_logits",
    )(where, *operands)
    return (high, low), (send, keep)


def back_body(plan, group, s_ref, g_ref, high_ref, low_ref, *outs):
    core = s_ref[1]
    base = plan.pair_range(group)[0]
    some, ends = [], []
    for c in plan.pairs[group]:
        a, n = plan.chunks[c]
        h = n // 2
        for side in (core, 1 - core):
            some.append(g_ref[pl.ds(pl.multiple_of(a - base + side * h, ROWS8), h), :])
            ends.append((ends[-1] if ends else 0) + h)
    x = jnp.concatenate(some, axis=0)
    width = 2 * LANES
    for k in range(0, plan.block, width):
        w = min(width, plan.block - k)
        part = dot3(x, high_ref[:, k : k + w], low_ref[:, k : k + w], NN)
        for out, start, end in zip(outs, [0] + ends, ends):
            out[:, k : k + w] = part[start:end]


def back(plan, where, group, values, high, low):
    rows, block, feats = plan.rows, plan.block, plan.feats
    n_group = plan.pair_range(group)[1]
    outs, specs = [], []
    for c in plan.pairs[group]:
        h = plan.chunks[c][1] // 2
        outs += [jax.ShapeDtypeStruct((h, feats), F32)] * 2
        specs += [pl.BlockSpec((h, block), lambda p, s: (0, p))] * 2
    result = pl.pallas_call(
        functools.partial(back_body, plan, group),
        out_shape=outs,
        grid_spec=pltpu.PrefetchScalarGridSpec(
            num_scalar_prefetch=1,
            grid=(plan.nb,),
            in_specs=[
                pl.BlockSpec((n_group, rows), lambda p, s: (0, 0), pipeline_mode=pl.Buffered(1)),
                pl.BlockSpec((rows, block), lambda p, s: (0, p)),
                pl.BlockSpec((rows, block), lambda p, s: (0, p)),
            ],
            out_specs=specs,
        ),
        compiler_params=params(20),
        cost_estimate=pl.CostEstimate(
            flops=6 * n_group * rows * feats, bytes_accessed=4 * feats * (rows + n_group), transcendentals=0
        ),
        name="back_group",
    )(where, values, high, low)
    return [tuple(result[2 * k : 2 * k + 2]) for k in range(len(plan.pairs[group]))]


class Pieces:
    def __init__(self, places, mine, theirs):
        self.places = (places, [tuple(p for place in places for p in place)])
        self.mine, self.theirs = mine, theirs

    def flat(self):
        return list(self.mine) + [self.theirs]


def gather_rows(plan, pair, chunks, s_ref, refs, position, target):
    core = s_ref[1]
    base = plan.pair_range(pair)[0]
    refs = list(refs)
    for c, places in zip(plan.pairs[pair], chunks):
        a, n = plan.chunks[c]
        h = n // 2
        for side, some in zip((core, 1 - core), places):
            for place in some:
                ref = refs.pop(0)
                if position in place:
                    k = place.index(position) * plan.block
                    target[pl.ds(pl.multiple_of(a - base + side * h, ROWS8), h), :] = ref[:, k : k + plan.block]


def forth_body(plan, pair, step, chunks, s_ref, *refs):
    nb = plan.nb
    refs = list(refs)
    scalar_ref = refs.pop(0) if step else None
    n_pieces = sum(len(some) for places in chunks for some in places)
    pieces, refs = refs[:n_pieces], refs[n_pieces:]
    direction_ref = refs.pop(0) if step else None
    high_ref, low_ref = refs[:2]
    n_ranges = len(tangent_ranges(plan, pair))
    target, acc, sums = refs[-3:]
    vector_ref, outs = refs[-4 - 2 * n_ranges], refs[-3 - 2 * n_ranges : -3]
    n_pair = plan.pair_range(pair)[1]
    p = pl.program_id(0)
    for position in range(nb):

        @pl.when(p == position)
        def _():
            gather_rows(plan, pair, chunks, s_ref, pieces, position, target)

    if step:
        direction = direction_ref[...]
        vector = direction - scalar_ref[0] * (target[...] + damping * direction)
    else:
        vector = -target[...]
    vector_ref[...] = vector
    part = dot3(vector, high_ref[...], low_ref[...], NT)
    square = jnp.sum(vector * vector).reshape(1, 1)
    cross = jnp.sum(vector * direction).reshape(1, 1) if step else square
    ids = lax.broadcasted_iota(jnp.int32, (ROWS8, plan.rows), 0)
    new = jnp.where(ids == 0, square, jnp.where(ids == 1, cross, 0.0))

    @pl.when(p == 0)
    def _():
        acc[:n_pair, :] = part
        sums[...] = new

    @pl.when(p > 0)
    def _():
        acc[:n_pair, :] += part
        sums[...] += new

    @pl.when(p == nb - 1)
    def _():
        acc[n_pair:, :] = sums[...]
        half = plan.rows // 2
        bit = s_ref[2]
        keep = pl.multiple_of(bit * half, LANES)
        send = pl.multiple_of((1 - bit) * half, LANES)
        for k, (a, n) in enumerate(tangent_ranges(plan, pair)):
            outs[2 * k][...] = acc[a : a + n, pl.ds(send, half)]
            outs[2 * k + 1][...] = acc[a : a + n, pl.ds(keep, half)]


def tangent_ranges(plan, pair):
    return [(0, plan.pair_range(pair)[1] + ROWS8)]


def placed(plan, pair):
    base, n_pair = plan.pair_range(pair)
    return pl.BlockSpec(
        (pl.Element(n_pair), pl.Element(plan.block)), lambda p, s: (base, (p ^ s[0]) * plan.block)
    )


def forth(plan, where, pair, pieces, high, low, vectors, step=None, direction=None):
    rows, block, feats, nb = plan.rows, plan.block, plan.feats, plan.nb
    half = rows // 2
    n_pair = plan.pair_range(pair)[1]
    operands, in_specs = [], []
    if step is not None:
        operands.append(step.reshape(1))
        in_specs.append(pl.BlockSpec(memory_space=pltpu.SMEM))
    for piece in pieces:
        for x in piece.flat():
            operands.append(x)
            in_specs.append(pl.BlockSpec(x.shape, lambda p, s: (0, 0), pipeline_mode=pl.Buffered(1)))
    if step is not None:
        operands.append(direction)
        in_specs.append(placed(plan, pair))
    operands += [high, low]
    in_specs += [pl.BlockSpec((rows, block), lambda p, s: (0, p))] * 2
    aliases = {}
    if vectors is not None:
        aliases = {len(operands) + 1: 0}
        operands.append(vectors)
        in_specs.append(pl.BlockSpec(memory_space=pl.ANY))
    outs, specs = [jax.ShapeDtypeStruct((plan.classes, feats), F32)], [placed(plan, pair)]
    for _, n in tangent_ranges(plan, pair):
        outs += [jax.ShapeDtypeStruct((n, half), F32)] * 2
        specs += [pl.BlockSpec((n, half), lambda p, s: (0, 0))] * 2
    result = pl.pallas_call(
        functools.partial(forth_body, plan, pair, step is not None, [piece.places for piece in pieces]),
        out_shape=outs,
        grid_spec=pltpu.PrefetchScalarGridSpec(
            num_scalar_prefetch=1,
            grid=(nb,),
            in_specs=in_specs,
            out_specs=specs,
            scratch_shapes=[
                pltpu.VMEM((n_pair, block), F32),
                pltpu.VMEM((n_pair + ROWS8, rows), F32),
                pltpu.VMEM((ROWS8, rows), F32),
            ],
        ),
        input_output_aliases=aliases,
        compiler_params=params(30),
        cost_estimate=pl.CostEstimate(
            flops=6 * n_pair * rows * feats, bytes_accessed=4 * feats * (rows + 3 * n_pair), transcendentals=0
        ),
        name="forth_pair",
    )(where, *operands)
    return result[0], [tuple(result[1 + 2 * k : 3 + 2 * k]) for k in range(len(tangent_ranges(plan, pair)))]


def last_body(plan, pair, chunks, s_ref, scalar_ref, *refs):
    nb = plan.nb
    refs = list(refs)
    n_pieces = sum(len(some) for places in chunks for some in places)
    pieces = refs[:n_pieces]
    direction_ref, residual_ref = refs[n_pieces : n_pieces + 2]
    out_ref, target, along, ready, arrived, left = refs[-6:]
    base, n_pair = plan.pair_range(pair)

    def place(ref, position):
        column = pl.multiple_of((position ^ s_ref[0]) * plan.block, LANES)
        return ref.at[pl.ds(base, n_pair), pl.ds(column, plan.block)]

    reads = []
    for q in range(nb):
        reads.append(pltpu.make_async_copy(place(direction_ref, q), along.at[q], arrived.at[0, q]))
        reads.append(pltpu.make_async_copy(place(residual_ref, q), ready.at[q], arrived.at[1, q]))
    writes = [pltpu.make_async_copy(ready.at[q], place(out_ref, q), left.at[q]) for q in range(nb)]
    for read in reads:
        read.start()
    for q in range(nb):
        gather_rows(plan, pair, chunks, s_ref, pieces, q, target)
        reads[2 * q].wait()
        reads[2 * q + 1].wait()
        residual = ready[q]
        following = residual + scalar_ref[1] * along[q]
        ready[q] = residual - scalar_ref[0] * (target[...] + damping * following)
        writes[q].start()
    for write in writes:
        write.wait()


def last(plan, where, pair, scalars, pieces, direction, residual, out):
    block, nb = plan.block, plan.nb
    n_pair = plan.pair_range(pair)[1]
    operands, in_specs = [where, scalars], [pl.BlockSpec(memory_space=pltpu.SMEM)] * 2
    for piece in pieces:
        for x in piece.flat():
            operands.append(x)
            in_specs.append(pl.BlockSpec(memory_space=pltpu.VMEM))
    operands += [direction, residual]
    aliases = {}
    if out is not None:
        aliases = {len(operands): 0}
        operands.append(out)
    in_specs += [pl.BlockSpec(memory_space=pl.ANY)] * (len(operands) - len(in_specs))
    return pl.pallas_call(
        functools.partial(last_body, plan, pair, [piece.places for piece in pieces]),
        out_shape=jax.ShapeDtypeStruct((plan.classes, plan.feats), F32),
        in_specs=in_specs,
        out_specs=pl.BlockSpec(memory_space=pl.ANY),
        scratch_shapes=[
            pltpu.VMEM((n_pair, block), F32),
            pltpu.VMEM((nb, n_pair, block), F32),
            pltpu.VMEM((nb, n_pair, block), F32),
            pltpu.SemaphoreType.DMA((2, nb)),
            pltpu.SemaphoreType.DMA((nb,)),
        ],
        input_output_aliases=aliases,
        compiler_params=params(22),
        cost_estimate=pl.CostEstimate(
            flops=6 * n_pair * plan.feats, bytes_accessed=16 * n_pair * plan.feats, transcendentals=0
        ),
        name="last_rows",
    )(*operands)


class Order:
    def __init__(self):
        self.token = None

    def after(self, x):
        if self.token is None:
            return x
        return lax.optimization_barrier((x, self.token))[0]

    def note(self, x):
        self.token = x


def columns(plan, x, positions):
    if list(positions) == list(range(positions[0], positions[-1] + 1)):
        return x[:, positions[0] * plan.block : (positions[-1] + 1) * plan.block]
    return jnp.concatenate([x[:, p * plan.block : (p + 1) * plan.block] for p in positions], axis=1)


class ClipSum:
    def __init__(self, plan, sides, turns):
        self.plan = plan
        self.own, other = sides
        levels = [(stride, 1 << k) for k, stride in enumerate(plan.levels)]
        down, up = (levels[::-1] if turn else levels for turn in turns)
        self.active = list(range(plan.nb))
        self.places, self.mine = [], []
        self.steps = [("core", 1, 0)]
        self.steps += [("scatter", stride, bit) for stride, bit in down]
        self.steps += [("double", stride, 0) for stride in plan.doubled]
        self.steps += [("gather", stride, bit) for stride, bit in up]
        self.kept = self.own
        self.pending = swap(other, "clip", 1)

    def done(self):
        return not self.steps

    def advance(self, order):
        kind, _, bit = self.steps.pop(0)
        got = order.after(self.pending)
        if kind == "gather":
            self.mine.append(got)
            self.places.append(tuple(p | bit for place in self.places for p in place))
        else:
            self.own = self.kept + got
            if not self.steps or self.steps[0][0] == "gather":
                self.places, self.mine = [tuple(self.active)], [self.own]
        kind, stride, bit = self.steps[0] if self.steps else ("core", 1, 0)
        if kind == "scatter":
            rest = [p for p in self.active if not p & bit]
            sent = columns(self.plan, self.own, [self.active.index(p | bit) for p in rest])
            self.kept = columns(self.plan, self.own, [self.active.index(p) for p in rest])
            self.active = rest
        elif kind == "double":
            sent = self.kept = self.own
        else:
            sent = self.mine[0] if len(self.mine) == 1 else jnp.concatenate(self.mine, axis=1)
        order.note(sent)
        self.pending = swap(sent, "clip", stride)

    def pieces(self, order):
        while not self.done():
            self.advance(order)
        return Pieces(self.places, self.mine, order.after(self.pending))


class FeatSum:
    def __init__(self, plan, halves, bit, axis):
        send, self.kept = halves
        self.bit, self.axis = bit, axis
        strides = [1 << k for k in range(plan.n_feat.bit_length() - 1)]
        self.strides = strides + [1]
        self.pending = swap(send, "feat", 1)

    def advance(self, order):
        self.strides.pop(0)
        got = order.after(self.pending)
        if self.strides:
            self.kept = self.kept + got
            self.pending = swap(self.kept, "feat", self.strides[0])
            order.note(self.kept)
        else:
            self.got = got
            order.note(got)

    def result(self, order):
        while self.strides:
            self.advance(order)
        one, two = [self.got, self.kept], [self.kept, self.got]
        return jnp.where(self.bit, jnp.concatenate(one, self.axis), jnp.concatenate(two, self.axis))


class ScalarSum:
    def __init__(self, plan, value):
        self.strides = [1 << k for k in range(plan.n_clip.bit_length() - 1)]
        self.row = jnp.broadcast_to(value, (ROWS8, LANES))
        self.pending = swap(self.row, "clip", 1)

    def advance(self, order):
        if not self.strides:
            return
        self.strides.pop(0)
        self.row = self.row + order.after(self.pending)
        order.note(self.row)
        if self.strides:
            self.pending = swap(self.row, "clip", self.strides[0])

    def result(self, order):
        while self.strides:
            self.advance(order)
        return self.row[0, 0]


def local(features, weights, labels):
    rows, feats = features.shape
    classes = weights.shape[0]
    plan = Plan(rows, feats, classes, lax.axis_size("clip"), lax.axis_size("feat"))
    total_rows = rows * plan.n_clip
    me, bit = lax.axis_index("clip"), lax.axis_index("feat") & 1
    mask = sum(((me // stride) & 1) << k for k, stride in enumerate(plan.levels))
    where = jnp.stack([jnp.asarray(mask), me & 1, bit]).astype(jnp.int32)
    order = Order()
    groups = range(len(plan.pairs))

    split, parts = None, []
    for part in range(rows // plan.rows_step):
        if part > 1:
            parts[part - 2].advance(order)
        split, halves = first(plan, where, order.after(features), weights, part, split)
        order.note(halves[0])
        parts.append(FeatSum(plan, halves, bit, 0))
    for summed in parts:
        summed.advance(order)
    high, low = split
    probs, values = [], []
    for part, summed in enumerate(parts):
        logits = summed.result(order)
        top = jnp.max(logits, axis=0, keepdims=True)
        powers = jnp.exp(logits - top)
        some = powers / jnp.sum(powers, axis=0, keepdims=True)
        mine = labels[part * plan.rows_step : (part + 1) * plan.rows_step]
        onehot = (mine[None, :] == jnp.arange(classes, dtype=jnp.int32)[:, None]).astype(F32)
        probs.append(some)
        values.append((some - onehot) / total_rows)
    probs, values = jnp.concatenate(probs, axis=1), jnp.concatenate(values, axis=1)

    def backward(values, scalar=None, during=None, under=None):
        sums, result = [None] * len(plan.chunks), None

        def multiply(group):
            a, n = plan.pair_range(group)
            sides = back(plan, where, group, order.after(values[a : a + n]), high, low)
            for c, side in zip(plan.pairs[group], sides):
                sums[c] = ClipSum(plan, side, plan.turns[c])
            order.note(sides[-1][0])

        def go(*chunks):
            for c in chunks:
                if not sums[c].done():
                    sums[c].advance(order)

        multiply(0)
        if scalar is not None:
            scalar.advance(order)
        go(0, 1)
        multiply(1)
        if scalar is not None:
            scalar.advance(order)
        go(0, 1, 2, 3)
        if scalar is not None:
            result = during(scalar.result(order))
        if under is not None:
            result = under(result)
        go(0, 1, 2, 3, 0, 1, 2, 3, 2, 3, 0, 1)
        return sums, go, result

    def forward(sums, go, step=None, direction=None):
        vectors, found = None, []

        def multiply(group):
            pieces = [sums[c].pieces(order) for c in plan.pairs[group]]
            out, halves = forth(plan, where, group, pieces, high, low, vectors, step, direction)
            order.note(halves[0][0])
            found.append(FeatSum(plan, halves[0], bit, 1))
            return out

        vectors = multiply(0)
        go(2, 3)
        found[0].advance(order)
        vectors = multiply(1)
        for k in (0, 1, 0, 1):
            if found[k].strides:
                found[k].advance(order)
        tangents = [f.result(order) for f in found]
        inner = sum(t[-ROWS8 : 2 - ROWS8, 0] for t in tangents)
        return vectors, jnp.concatenate([t[:-ROWS8] for t in tangents], axis=0), inner

    def bend(tangent):
        weighted = probs * tangent
        bent = (weighted - probs * jnp.sum(weighted, axis=0, keepdims=True)) / total_rows
        order.note(bent)
        return bent, ScalarSum(plan, jnp.sum(bent * tangent))

    sums, go, _ = backward(values)
    direction, tangent, inner = forward(sums, go)
    norm0 = inner[0]
    bent, curvature = bend(tangent)

    sums, go, step0 = backward(bent, curvature, lambda total: norm0 / (total + damping * norm0))
    residual, fresh, inner = forward(sums, go, step0, direction)
    norm1, cross = inner[0], inner[1]
    ratio = norm1 / norm0
    bent, curvature = bend(fresh + ratio * tangent)
    length = norm1 + 2.0 * ratio * cross + ratio * ratio * norm0

    def under(step1):
        moved = order.after(weights) + (step0 + step1 * ratio) * direction + step1 * residual
        order.note(moved)
        return step1, moved

    sums, go, (step1, moved) = backward(
        bent, curvature, lambda total: norm1 / (total + damping * length), under
    )
    scalars, out = jnp.stack([step1, ratio]), None
    for group, members in enumerate(plan.pairs):
        pieces = [sums[c].pieces(order) for c in members]
        if group == 0:
            go(2, 3)
        out = last(plan, where, group, scalars, pieces, direction, residual, out)
        order.note(out)
    return moved, out


def solution(mesh):
    in_specs = (P("clip", "feat"), P(None, "feat"), P("clip"))
    out_specs = (P(None, "feat"), P(None, "feat"))
    return jax.shard_map(local, mesh=mesh, in_specs=in_specs, out_specs=out_specs, check_vma=False)
```

```python
import functools

import jax
import jax.numpy as jnp
from jax import lax
from jax.experimental import pallas as pl
from jax.experimental.pallas import tpu as pltpu
from jax.sharding import PartitionSpec as P

damping = 0.01
F32, BF16 = jnp.float32, jnp.bfloat16
LANES, ROWS8, UNIT = 128, 8, 16
NT = (((1,), (1,)), ((), ()))
NN = (((1,), (0,)), ((), ()))
MIB = 1024 * 1024


def parts_of(x):
    high = x.astype(BF16)
    return high, (x - high.astype(F32)).astype(BF16)


def dot3(x, high, low, dims):
    x_high, x_low = parts_of(x)
    dot = functools.partial(lax.dot_general, dimension_numbers=dims, preferred_element_type=F32)
    return dot(x_high, high) + (dot(x_low, high) + dot(x_high, low))


def params(mib):
    return pltpu.CompilerParams(vmem_limit_bytes=mib * MIB)


class Plan:
    def __init__(self, rows, feats, classes, n_clip, n_feat):
        self.rows, self.feats, self.classes = rows, feats, classes
        self.n_clip, self.n_feat = n_clip, n_feat
        units = classes // UNIT
        small = units // 5
        middle = (units - 2 * small) // 2
        sizes = [UNIT * k for k in (units - 2 * small - middle, middle, small, small)]
        starts = [sum(sizes[:k]) for k in range(4)]
        self.chunks = list(zip(starts, sizes))
        self.pairs = [(0, 1), (2, 3)]
        self.turns = [(0, 1), (1, 0), (0, 1), (1, 0)]
        strides = [1 << k for k in range(1, n_clip.bit_length() - 1)]
        self.levels, block = [], feats
        while strides and block % (2 * LANES) == 0:
            self.levels.append(strides.pop(0))
            block //= 2
        self.doubled = strides
        self.block, self.nb = block, feats // block
        self.rows_step = next(n for n in (256, 128, rows) if rows % n == 0)

    def pair_range(self, pair):
        first, last = self.pairs[pair][0], self.pairs[pair][-1]
        start = self.chunks[first][0]
        return start, self.chunks[last][0] + self.chunks[last][1] - start


def swap(x, axis, stride):
    size = lax.axis_size(axis)
    return lax.ppermute(x, axis, [(i, i ^ stride) for i in range(size)])


def first_body(plan, s_ref, f_ref, w_ref, *rest):
    high_ref, low_ref, send_ref, keep_ref, acc = rest[-5:]
    p = pl.program_id(0)
    high, low = parts_of(f_ref[...])
    high_ref[...] = high
    low_ref[...] = low
    part = dot3(w_ref[...], high, low, NT)

    @pl.when(p == 0)
    def _():
        acc[...] = part

    @pl.when(p > 0)
    def _():
        acc[...] += part

    @pl.when(p == plan.nb - 1)
    def _():
        half = plan.classes // 2
        bit = s_ref[2]
        send_ref[...] = acc[pl.ds(pl.multiple_of((1 - bit) * half, ROWS8), half), :]
        keep_ref[...] = acc[pl.ds(pl.multiple_of(bit * half, ROWS8), half), :]


def first(plan, where, features, weights, part, split):
    rows, block, step = plan.rows, plan.block, plan.rows_step
    half = plan.classes // 2
    operands = [features, weights]
    in_specs = [
        pl.BlockSpec((step, block), lambda p, s: (part, p ^ s[0])),
        pl.BlockSpec((plan.classes, block), lambda p, s: (0, p ^ s[0])),
    ]
    aliases = {}
    if split is not None:
        aliases = {3: 0, 4: 1}
        operands += list(split)
        in_specs += [pl.BlockSpec(memory_space=pltpu.HBM)] * 2
    high, low, send, keep = pl.pallas_call(
        functools.partial(first_body, plan),
        out_shape=[pltpu.HBM((rows, plan.feats), BF16)] * 2
        + [jax.ShapeDtypeStruct((half, step), F32)] * 2,
        grid_spec=pltpu.PrefetchScalarGridSpec(
            num_scalar_prefetch=1,
            grid=(plan.nb,),
            in_specs=in_specs,
            out_specs=[pl.BlockSpec((step, block), lambda p, s: (part, p))] * 2
            + [pl.BlockSpec((half, step), lambda p, s: (0, 0))] * 2,
            scratch_shapes=[pltpu.VMEM((plan.classes, step), F32)],
        ),
        input_output_aliases=aliases,
        compiler_params=params(56),
        cost_estimate=pl.CostEstimate(
            flops=6 * plan.classes * step * plan.feats,
            bytes_accessed=4 * plan.feats * (2 * step + plan.classes),
            transcendentals=0,
        ),
        name="split_and_logits",
    )(where, *operands)
    return (high, low), (send, keep)


def stream(plan, p, sources, buffers, sems):
    def copies(step):
        slot = lax.rem(step, 2)
        place = pl.ds(pl.multiple_of(step * plan.block, LANES), plan.block)
        return [
            pltpu.make_async_copy(source.at[:, place], buffer.at[slot], sems.at[k, slot])
            for k, (source, buffer) in enumerate(zip(sources, buffers))
        ]

    @pl.when(p == 0)
    def _():
        for copy in copies(p):
            copy.start()

    @pl.when(p + 1 < plan.nb)
    def _():
        for copy in copies(p + 1):
            copy.start()

    for copy in copies(p):
        copy.wait()
    return [buffer.at[lax.rem(p, 2)] for buffer in buffers]


def stream_scratch(plan):
    buffer = pltpu.VMEM((2, plan.rows, plan.block), BF16)
    return [buffer, buffer, pltpu.SemaphoreType.DMA((2, 2))]


def back_body(plan, group, s_ref, g_ref, high_hbm, low_hbm, *rest):
    outs, (high_buf, low_buf, sems) = rest[:-5], rest[-3:]
    high_ref, low_ref = stream(plan, pl.program_id(0), (high_hbm, low_hbm), (high_buf, low_buf), sems)
    core = s_ref[1]
    base = plan.pair_range(group)[0]
    some, ends = [], []
    for c in plan.pairs[group]:
        a, n = plan.chunks[c]
        h = n // 2
        for side in (core, 1 - core):
            some.append(g_ref[pl.ds(pl.multiple_of(a - base + side * h, ROWS8), h), :])
            ends.append((ends[-1] if ends else 0) + h)
    x = jnp.concatenate(some, axis=0)
    width = 2 * LANES
    for k in range(0, plan.block, width):
        w = min(width, plan.block - k)
        part = dot3(x, high_ref[:, k : k + w], low_ref[:, k : k + w], NN)
        for out, start, end in zip(outs, [0] + ends, ends):
            out[:, k : k + w] = part[start:end]


def back(plan, where, group, values, high, low):
    rows, block, feats = plan.rows, plan.block, plan.feats
    n_group = plan.pair_range(group)[1]
    outs, specs = [], []
    for c in plan.pairs[group]:
        h = plan.chunks[c][1] // 2
        outs += [jax.ShapeDtypeStruct((h, feats), F32)] * 2
        specs += [pl.BlockSpec((h, block), lambda p, s: (0, p))] * 2
    aliases = {2: len(outs), 3: len(outs) + 1}
    outs += [pltpu.HBM((rows, feats), BF16)] * 2
    specs += [pl.BlockSpec(memory_space=pltpu.HBM)] * 2
    result = pl.pallas_call(
        functools.partial(back_body, plan, group),
        out_shape=outs,
        grid_spec=pltpu.PrefetchScalarGridSpec(
            num_scalar_prefetch=1,
            grid=(plan.nb,),
            in_specs=[
                pl.BlockSpec((n_group, rows), lambda p, s: (0, 0), pipeline_mode=pl.Buffered(1)),
                pl.BlockSpec(memory_space=pltpu.HBM),
                pl.BlockSpec(memory_space=pltpu.HBM),
            ],
            out_specs=specs,
            scratch_shapes=stream_scratch(plan),
        ),
        input_output_aliases=aliases,
        compiler_params=params(20),
        cost_estimate=pl.CostEstimate(
            flops=6 * n_group * rows * feats, bytes_accessed=4 * feats * (rows + n_group), transcendentals=0
        ),
        name="back_group",
    )(where, values, high, low)
    return [tuple(result[2 * k : 2 * k + 2]) for k in range(len(plan.pairs[group]))], tuple(result[-2:])


class Pieces:
    def __init__(self, places, mine, theirs):
        self.places = (places, [tuple(p for place in places for p in place)])
        self.mine, self.theirs = mine, theirs

    def flat(self):
        return list(self.mine) + [self.theirs]


def gather_rows(plan, pair, chunks, s_ref, refs, position, target):
    core = s_ref[1]
    base = plan.pair_range(pair)[0]
    refs = list(refs)
    for c, places in zip(plan.pairs[pair], chunks):
        a, n = plan.chunks[c]
        h = n // 2
        for side, some in zip((core, 1 - core), places):
            for place in some:
                ref = refs.pop(0)
                if position in place:
                    k = place.index(position) * plan.block
                    target[pl.ds(pl.multiple_of(a - base + side * h, ROWS8), h), :] = ref[:, k : k + plan.block]


def forth_body(plan, pair, step, chunks, s_ref, *refs):
    nb = plan.nb
    refs = list(refs)
    scalar_ref = refs.pop(0) if step else None
    n_pieces = sum(len(some) for places in chunks for some in places)
    pieces, refs = refs[:n_pieces], refs[n_pieces:]
    direction_ref = refs.pop(0) if step else None
    high_hbm, low_hbm = refs[:2]
    n_ranges = len(tangent_ranges(plan, pair))
    target, acc, sums, high_buf, low_buf, sems = refs[-6:]
    vector_ref, outs = refs[-9 - 2 * n_ranges], refs[-8 - 2 * n_ranges : -8]
    n_pair = plan.pair_range(pair)[1]
    p = pl.program_id(0)
    high_ref, low_ref = stream(plan, p, (high_hbm, low_hbm), (high_buf, low_buf), sems)
    for position in range(nb):

        @pl.when(p == position)
        def _():
            gather_rows(plan, pair, chunks, s_ref, pieces, position, target)

    if step:
        direction = direction_ref[...]
        vector = direction - scalar_ref[0] * (target[...] + damping * direction)
    else:
        vector = -target[...]
    vector_ref[...] = vector
    part = dot3(vector, high_ref[...], low_ref[...], NT)
    square = jnp.sum(vector * vector).reshape(1, 1)
    cross = jnp.sum(vector * direction).reshape(1, 1) if step else square
    ids = lax.broadcasted_iota(jnp.int32, (ROWS8, plan.rows), 0)
    new = jnp.where(ids == 0, square, jnp.where(ids == 1, cross, 0.0))

    @pl.when(p == 0)
    def _():
        acc[:n_pair, :] = part
        sums[...] = new

    @pl.when(p > 0)
    def _():
        acc[:n_pair, :] += part
        sums[...] += new

    @pl.when(p == nb - 1)
    def _():
        acc[n_pair:, :] = sums[...]
        half = plan.rows // 2
        bit = s_ref[2]
        keep = pl.multiple_of(bit * half, LANES)
        send = pl.multiple_of((1 - bit) * half, LANES)
        for k, (a, n) in enumerate(tangent_ranges(plan, pair)):
            outs[2 * k][...] = acc[a : a + n, pl.ds(send, half)]
            outs[2 * k + 1][...] = acc[a : a + n, pl.ds(keep, half)]


def tangent_ranges(plan, pair):
    return [(0, plan.pair_range(pair)[1] + ROWS8)]


def placed(plan, pair):
    base, n_pair = plan.pair_range(pair)
    return pl.BlockSpec(
        (pl.Element(n_pair), pl.Element(plan.block)), lambda p, s: (base, (p ^ s[0]) * plan.block)
    )


def forth(plan, where, pair, pieces, high, low, vectors, step=None, direction=None):
    rows, block, feats, nb = plan.rows, plan.block, plan.feats, plan.nb
    half = rows // 2
    n_pair = plan.pair_range(pair)[1]
    operands, in_specs = [], []
    if step is not None:
        operands.append(step.reshape(1))
        in_specs.append(pl.BlockSpec(memory_space=pltpu.SMEM))
    for piece in pieces:
        for x in piece.flat():
            operands.append(x)
            in_specs.append(pl.BlockSpec(x.shape, lambda p, s: (0, 0), pipeline_mode=pl.Buffered(1)))
    if step is not None:
        operands.append(direction)
        in_specs.append(placed(plan, pair))
    n_ranges = len(tangent_ranges(plan, pair))
    aliases = {len(operands) + 1: 1 + 2 * n_ranges, len(operands) + 2: 2 + 2 * n_ranges}
    operands += [high, low]
    in_specs += [pl.BlockSpec(memory_space=pltpu.HBM)] * 2
    if vectors is not None:
        aliases[len(operands) + 1] = 0
        operands.append(vectors)
        in_specs.append(pl.BlockSpec(memory_space=pl.ANY))
    outs, specs = [pltpu.HBM((plan.classes, feats), F32)], [placed(plan, pair)]
    for _, n in tangent_ranges(plan, pair):
        outs += [jax.ShapeDtypeStruct((n, half), F32)] * 2
        specs += [pl.BlockSpec((n, half), lambda p, s: (0, 0))] * 2
    outs += [pltpu.HBM((rows, feats), BF16)] * 2
    specs += [pl.BlockSpec(memory_space=pltpu.HBM)] * 2
    result = pl.pallas_call(
        functools.partial(forth_body, plan, pair, step is not None, [piece.places for piece in pieces]),
        out_shape=outs,
        grid_spec=pltpu.PrefetchScalarGridSpec(
            num_scalar_prefetch=1,
            grid=(nb,),
            in_specs=in_specs,
            out_specs=specs,
            scratch_shapes=[
                pltpu.VMEM((n_pair, block), F32),
                pltpu.VMEM((n_pair + ROWS8, rows), F32),
                pltpu.VMEM((ROWS8, rows), F32),
            ]
            + stream_scratch(plan),
        ),
        input_output_aliases=aliases,
        compiler_params=params(30),
        cost_estimate=pl.CostEstimate(
            flops=6 * n_pair * rows * feats, bytes_accessed=4 * feats * (rows + 3 * n_pair), transcendentals=0
        ),
        name="forth_pair",
    )(where, *operands)
    return result[0], [tuple(result[1 + 2 * k : 3 + 2 * k]) for k in range(n_ranges)], tuple(result[-2:])


def last_body(plan, pair, chunks, s_ref, scalar_ref, *refs):
    nb = plan.nb
    refs = list(refs)
    n_pieces = sum(len(some) for places in chunks for some in places)
    pieces = refs[:n_pieces]
    direction_ref, residual_ref = refs[n_pieces : n_pieces + 2]
    out_ref, target, along, ready, arrived, left = refs[-6:]
    base, n_pair = plan.pair_range(pair)

    def place(ref, position):
        column = pl.multiple_of((position ^ s_ref[0]) * plan.block, LANES)
        return ref.at[pl.ds(base, n_pair), pl.ds(column, plan.block)]

    reads = []
    for q in range(nb):
        reads.append(pltpu.make_async_copy(place(direction_ref, q), along.at[q], arrived.at[0, q]))
        reads.append(pltpu.make_async_copy(place(residual_ref, q), ready.at[q], arrived.at[1, q]))
    writes = [pltpu.make_async_copy(ready.at[q], place(out_ref, q), left.at[q]) for q in range(nb)]
    for read in reads:
        read.start()
    for q in range(nb):
        gather_rows(plan, pair, chunks, s_ref, pieces, q, target)
        reads[2 * q].wait()
        reads[2 * q + 1].wait()
        residual = ready[q]
        following = residual + scalar_ref[1] * along[q]
        ready[q] = residual - scalar_ref[0] * (target[...] + damping * following)
        writes[q].start()
    for write in writes:
        write.wait()


def last(plan, where, pair, scalars, pieces, direction, residual, out):
    block, nb = plan.block, plan.nb
    n_pair = plan.pair_range(pair)[1]
    operands, in_specs = [where, scalars], [pl.BlockSpec(memory_space=pltpu.SMEM)] * 2
    for piece in pieces:
        for x in piece.flat():
            operands.append(x)
            in_specs.append(pl.BlockSpec(memory_space=pltpu.VMEM))
    operands += [direction, residual]
    aliases = {}
    if out is not None:
        aliases = {len(operands): 0}
        operands.append(out)
    in_specs += [pl.BlockSpec(memory_space=pl.ANY)] * (len(operands) - len(in_specs))
    return pl.pallas_call(
        functools.partial(last_body, plan, pair, [piece.places for piece in pieces]),
        out_shape=jax.ShapeDtypeStruct((plan.classes, plan.feats), F32),
        in_specs=in_specs,
        out_specs=pl.BlockSpec(memory_space=pl.ANY),
        scratch_shapes=[
            pltpu.VMEM((n_pair, block), F32),
            pltpu.VMEM((nb, n_pair, block), F32),
            pltpu.VMEM((nb, n_pair, block), F32),
            pltpu.SemaphoreType.DMA((2, nb)),
            pltpu.SemaphoreType.DMA((nb,)),
        ],
        input_output_aliases=aliases,
        compiler_params=params(22),
        cost_estimate=pl.CostEstimate(
            flops=6 * n_pair * plan.feats, bytes_accessed=16 * n_pair * plan.feats, transcendentals=0
        ),
        name="last_rows",
    )(*operands)


class Order:
    def __init__(self):
        self.token = None

    def after(self, x):
        if self.token is None:
            return x
        return lax.optimization_barrier((x, self.token))[0]

    def note(self, x):
        self.token = x


def columns(plan, x, positions):
    if list(positions) == list(range(positions[0], positions[-1] + 1)):
        return x[:, positions[0] * plan.block : (positions[-1] + 1) * plan.block]
    return jnp.concatenate([x[:, p * plan.block : (p + 1) * plan.block] for p in positions], axis=1)


class ClipSum:
    def __init__(self, plan, sides, turns):
        self.plan = plan
        self.own, other = sides
        levels = [(stride, 1 << k) for k, stride in enumerate(plan.levels)]
        down, up = (levels[::-1] if turn else levels for turn in turns)
        self.active = list(range(plan.nb))
        self.places, self.mine = [], []
        self.steps = [("core", 1, 0)]
        self.steps += [("scatter", stride, bit) for stride, bit in down]
        self.steps += [("double", stride, 0) for stride in plan.doubled]
        self.steps += [("gather", stride, bit) for stride, bit in up]
        self.kept = self.own
        self.pending = swap(other, "clip", 1)

    def done(self):
        return not self.steps

    def advance(self, order):
        kind, _, bit = self.steps.pop(0)
        got = order.after(self.pending)
        if kind == "gather":
            self.mine.append(got)
            self.places.append(tuple(p | bit for place in self.places for p in place))
        else:
            self.own = self.kept + got
            if not self.steps or self.steps[0][0] == "gather":
                self.places, self.mine = [tuple(self.active)], [self.own]
        kind, stride, bit = self.steps[0] if self.steps else ("core", 1, 0)
        if kind == "scatter":
            rest = [p for p in self.active if not p & bit]
            sent = columns(self.plan, self.own, [self.active.index(p | bit) for p in rest])
            self.kept = columns(self.plan, self.own, [self.active.index(p) for p in rest])
            self.active = rest
        elif kind == "double":
            sent = self.kept = self.own
        else:
            sent = self.mine[0] if len(self.mine) == 1 else jnp.concatenate(self.mine, axis=1)
        order.note(sent)
        self.pending = swap(sent, "clip", stride)

    def pieces(self, order):
        while not self.done():
            self.advance(order)
        return Pieces(self.places, self.mine, order.after(self.pending))


class FeatSum:
    def __init__(self, plan, halves, bit, axis):
        send, self.kept = halves
        self.bit, self.axis = bit, axis
        strides = [1 << k for k in range(plan.n_feat.bit_length() - 1)]
        self.strides = strides + [1]
        self.pending = swap(send, "feat", 1)

    def advance(self, order):
        self.strides.pop(0)
        got = order.after(self.pending)
        if self.strides:
            self.kept = self.kept + got
            self.pending = swap(self.kept, "feat", self.strides[0])
            order.note(self.kept)
        else:
            self.got = got
            order.note(got)

    def result(self, order):
        while self.strides:
            self.advance(order)
        one, two = [self.got, self.kept], [self.kept, self.got]
        return jnp.where(self.bit, jnp.concatenate(one, self.axis), jnp.concatenate(two, self.axis))


class ScalarSum:
    def __init__(self, plan, value):
        self.strides = [1 << k for k in range(plan.n_clip.bit_length() - 1)]
        self.row = jnp.broadcast_to(value, (ROWS8, LANES))
        self.pending = swap(self.row, "clip", 1)

    def advance(self, order):
        if not self.strides:
            return
        self.strides.pop(0)
        self.row = self.row + order.after(self.pending)
        order.note(self.row)
        if self.strides:
            self.pending = swap(self.row, "clip", self.strides[0])

    def result(self, order):
        while self.strides:
            self.advance(order)
        return self.row[0, 0]


def local(features, weights, labels):
    rows, feats = features.shape
    classes = weights.shape[0]
    plan = Plan(rows, feats, classes, lax.axis_size("clip"), lax.axis_size("feat"))
    total_rows = rows * plan.n_clip
    me, bit = lax.axis_index("clip"), lax.axis_index("feat") & 1
    mask = sum(((me // stride) & 1) << k for k, stride in enumerate(plan.levels))
    where = jnp.stack([jnp.asarray(mask), me & 1, bit]).astype(jnp.int32)
    order = Order()
    groups = range(len(plan.pairs))

    split, parts = None, []
    for part in range(rows // plan.rows_step):
        if part > 1:
            parts[part - 2].advance(order)
        split, halves = first(plan, where, order.after(features), weights, part, split)
        order.note(halves[0])
        parts.append(FeatSum(plan, halves, bit, 0))
    for summed in parts:
        summed.advance(order)
    split = list(split)
    probs, values = [], []
    for part, summed in enumerate(parts):
        logits = summed.result(order)
        top = jnp.max(logits, axis=0, keepdims=True)
        powers = jnp.exp(logits - top)
        some = powers / jnp.sum(powers, axis=0, keepdims=True)
        mine = labels[part * plan.rows_step : (part + 1) * plan.rows_step]
        onehot = (mine[None, :] == jnp.arange(classes, dtype=jnp.int32)[:, None]).astype(F32)
        probs.append(some)
        values.append((some - onehot) / total_rows)
    probs, values = jnp.concatenate(probs, axis=1), jnp.concatenate(values, axis=1)

    def backward(values, scalar=None, during=None, under=None):
        sums, result = [None] * len(plan.chunks), None

        def multiply(group):
            a, n = plan.pair_range(group)
            sides, split[:] = back(plan, where, group, order.after(values[a : a + n]), *split)
            for c, side in zip(plan.pairs[group], sides):
                sums[c] = ClipSum(plan, side, plan.turns[c])
            order.note(sides[-1][0])

        def go(*chunks):
            for c in chunks:
                if not sums[c].done():
                    sums[c].advance(order)

        multiply(0)
        if scalar is not None:
            scalar.advance(order)
        go(0, 1)
        multiply(1)
        if scalar is not None:
            scalar.advance(order)
        go(0, 1, 2, 3)
        if scalar is not None:
            result = during(scalar.result(order))
        if under is not None:
            result = under(result)
        go(0, 1, 2, 3, 0, 1, 2, 3, 2, 3, 0, 1)
        return sums, go, result

    def forward(sums, go, step=None, direction=None):
        vectors, found = None, []

        def multiply(group):
            pieces = [sums[c].pieces(order) for c in plan.pairs[group]]
            out, halves, split[:] = forth(plan, where, group, pieces, *split, vectors, step, direction)
            order.note(halves[0][0])
            found.append(FeatSum(plan, halves[0], bit, 1))
            return out

        vectors = multiply(0)
        go(2, 3)
        found[0].advance(order)
        vectors = multiply(1)
        for k in (0, 1, 0, 1):
            if found[k].strides:
                found[k].advance(order)
        tangents = [f.result(order) for f in found]
        inner = sum(t[-ROWS8 : 2 - ROWS8, 0] for t in tangents)
        return vectors, jnp.concatenate([t[:-ROWS8] for t in tangents], axis=0), inner

    def bend(tangent):
        weighted = probs * tangent
        bent = (weighted - probs * jnp.sum(weighted, axis=0, keepdims=True)) / total_rows
        order.note(bent)
        return bent, ScalarSum(plan, jnp.sum(bent * tangent))

    sums, go, _ = backward(values)
    direction, tangent, inner = forward(sums, go)
    norm0 = inner[0]
    bent, curvature = bend(tangent)

    sums, go, step0 = backward(bent, curvature, lambda total: norm0 / (total + damping * norm0))
    residual, fresh, inner = forward(sums, go, step0, direction)
    norm1, cross = inner[0], inner[1]
    ratio = norm1 / norm0
    bent, curvature = bend(fresh + ratio * tangent)
    length = norm1 + 2.0 * ratio * cross + ratio * ratio * norm0

    def under(step1):
        moved = order.after(weights) + (step0 + step1 * ratio) * direction + step1 * residual
        order.note(moved)
        return step1, moved

    sums, go, (step1, moved) = backward(
        bent, curvature, lambda total: norm1 / (total + damping * length), under
    )
    scalars, out = jnp.stack([step1, ratio]), None
    for group, members in enumerate(plan.pairs):
        pieces = [sums[c].pieces(order) for c in members]
        if group == 0:
            go(2, 3)
        out = last(plan, where, group, scalars, pieces, direction, residual, out)
        order.note(out)
    return moved, out


def solution(mesh):
    in_specs = (P("clip", "feat"), P(None, "feat"), P("clip"))
    out_specs = (P(None, "feat"), P(None, "feat"))
    return jax.shard_map(local, mesh=mesh, in_specs=in_specs, out_specs=out_specs, check_vma=False)
```

```python
import functools

import jax
import jax.numpy as jnp
from jax import lax
from jax.experimental import pallas as pl
from jax.experimental.pallas import tpu as pltpu
from jax.sharding import PartitionSpec as P

damping = 0.01
F32, BF16 = jnp.float32, jnp.bfloat16
LANES, ROWS8, UNIT = 128, 8, 16
NT = (((1,), (1,)), ((), ()))
NN = (((1,), (0,)), ((), ()))
MIB = 1024 * 1024


def parts_of(x):
    high = x.astype(BF16)
    return high, (x - high.astype(F32)).astype(BF16)


def dot3(x, high, low, dims):
    x_high, x_low = parts_of(x)
    dot = functools.partial(lax.dot_general, dimension_numbers=dims, preferred_element_type=F32)
    return dot(x_high, high) + (dot(x_low, high) + dot(x_high, low))


def params(mib):
    return pltpu.CompilerParams(vmem_limit_bytes=mib * MIB)


class Plan:
    def __init__(self, rows, feats, classes, n_clip, n_feat):
        self.rows, self.feats, self.classes = rows, feats, classes
        self.n_clip, self.n_feat = n_clip, n_feat
        units = classes // UNIT
        small = units // 5
        middle = (units - 2 * small) // 2
        sizes = [UNIT * k for k in (units - 2 * small - middle, middle, small, small)]
        starts = [sum(sizes[:k]) for k in range(4)]
        self.chunks = list(zip(starts, sizes))
        self.pairs = [(0, 1), (2, 3)]
        self.turns = [(0, 1), (1, 0), (0, 1), (1, 0)]
        strides = [1 << k for k in range(1, n_clip.bit_length() - 1)]
        self.levels, block = [], feats
        while strides and block % (2 * LANES) == 0:
            self.levels.append(strides.pop(0))
            block //= 2
        self.doubled = strides
        self.block, self.nb = block, feats // block
        self.rows_step = next(n for n in (256, 128, rows) if rows % n == 0)

    def pair_range(self, pair):
        first, last = self.pairs[pair][0], self.pairs[pair][-1]
        start = self.chunks[first][0]
        return start, self.chunks[last][0] + self.chunks[last][1] - start


def swap(x, axis, stride):
    size = lax.axis_size(axis)
    return lax.ppermute(x, axis, [(i, i ^ stride) for i in range(size)])


def first_body(plan, s_ref, f_ref, w_ref, *rest):
    high_ref, low_ref, send_ref, keep_ref, acc = rest[-5:]
    p = pl.program_id(0)
    high, low = parts_of(f_ref[...])
    high_ref[...] = high
    low_ref[...] = low
    part = dot3(w_ref[...], high, low, NT)

    @pl.when(p == 0)
    def _():
        acc[...] = part

    @pl.when(p > 0)
    def _():
        acc[...] += part

    @pl.when(p == plan.nb - 1)
    def _():
        half = plan.classes // 2
        bit = s_ref[2]
        send_ref[...] = acc[pl.ds(pl.multiple_of((1 - bit) * half, ROWS8), half), :]
        keep_ref[...] = acc[pl.ds(pl.multiple_of(bit * half, ROWS8), half), :]


def first(plan, where, features, weights, part, split):
    rows, block, step = plan.rows, plan.block, plan.rows_step
    half = plan.classes // 2
    operands = [features, weights]
    in_specs = [
        pl.BlockSpec((step, block), lambda p, s: (part, p ^ s[0])),
        pl.BlockSpec((plan.classes, block), lambda p, s: (0, p ^ s[0])),
    ]
    aliases = {}
    if split is not None:
        aliases = {3: 0, 4: 1}
        operands += list(split)
        in_specs += [pl.BlockSpec(memory_space=pltpu.HBM)] * 2
    high, low, send, keep = pl.pallas_call(
        functools.partial(first_body, plan),
        out_shape=[pltpu.HBM((rows, plan.feats), BF16)] * 2
        + [jax.ShapeDtypeStruct((half, step), F32)] * 2,
        grid_spec=pltpu.PrefetchScalarGridSpec(
            num_scalar_prefetch=1,
            grid=(plan.nb,),
            in_specs=in_specs,
            out_specs=[pl.BlockSpec((step, block), lambda p, s: (part, p))] * 2
            + [pl.BlockSpec((half, step), lambda p, s: (0, 0))] * 2,
            scratch_shapes=[pltpu.VMEM((plan.classes, step), F32)],
        ),
        input_output_aliases=aliases,
        compiler_params=params(56),
        cost_estimate=pl.CostEstimate(
            flops=6 * plan.classes * step * plan.feats,
            bytes_accessed=4 * plan.feats * (2 * step + plan.classes),
            transcendentals=0,
        ),
        name="split_and_logits",
    )(where, *operands)
    return (high, low), (send, keep)


def stream(plan, p, sources, buffers, sems):
    def copies(step):
        slot = lax.rem(step, 2)
        place = pl.ds(pl.multiple_of(step * plan.block, LANES), plan.block)
        return [
            pltpu.make_async_copy(source.at[:, place], buffer.at[slot], sems.at[k, slot])
            for k, (source, buffer) in enumerate(zip(sources, buffers))
        ]

    @pl.when(p == 0)
    def _():
        for copy in copies(p):
            copy.start()

    @pl.when(p + 1 < plan.nb)
    def _():
        for copy in copies(p + 1):
            copy.start()

    for copy in copies(p):
        copy.wait()
    return [buffer.at[lax.rem(p, 2)] for buffer in buffers]


def stream_scratch(plan):
    buffer = pltpu.VMEM((2, plan.rows, plan.block), BF16)
    return [buffer, buffer, pltpu.SemaphoreType.DMA((2, 2))]


def back_body(plan, group, s_ref, g_ref, high_hbm, low_hbm, *rest):
    outs, (high_buf, low_buf, sems) = rest[:-5], rest[-3:]
    high_ref, low_ref = stream(plan, pl.program_id(0), (high_hbm, low_hbm), (high_buf, low_buf), sems)
    core = s_ref[1]
    base = plan.pair_range(group)[0]
    some, ends = [], []
    for c in plan.pairs[group]:
        a, n = plan.chunks[c]
        h = n // 2
        for side in (core, 1 - core):
            some.append(g_ref[pl.ds(pl.multiple_of(a - base + side * h, ROWS8), h), :])
            ends.append((ends[-1] if ends else 0) + h)
    x = jnp.concatenate(some, axis=0)
    width = 2 * LANES
    for k in range(0, plan.block, width):
        w = min(width, plan.block - k)
        part = dot3(x, high_ref[:, k : k + w], low_ref[:, k : k + w], NN)
        for out, start, end in zip(outs, [0] + ends, ends):
            out[:, k : k + w] = part[start:end]


def back(plan, where, group, values, high, low):
    rows, block, feats = plan.rows, plan.block, plan.feats
    n_group = plan.pair_range(group)[1]
    outs, specs = [], []
    for c in plan.pairs[group]:
        h = plan.chunks[c][1] // 2
        outs += [jax.ShapeDtypeStruct((h, feats), F32)] * 2
        specs += [pl.BlockSpec((h, block), lambda p, s: (0, p))] * 2
    aliases = {2: len(outs), 3: len(outs) + 1}
    outs += [pltpu.HBM((rows, feats), BF16)] * 2
    specs += [pl.BlockSpec(memory_space=pltpu.HBM)] * 2
    result = pl.pallas_call(
        functools.partial(back_body, plan, group),
        out_shape=outs,
        grid_spec=pltpu.PrefetchScalarGridSpec(
            num_scalar_prefetch=1,
            grid=(plan.nb,),
            in_specs=[
                pl.BlockSpec((n_group, rows), lambda p, s: (0, 0), pipeline_mode=pl.Buffered(1)),
                pl.BlockSpec(memory_space=pltpu.HBM),
                pl.BlockSpec(memory_space=pltpu.HBM),
            ],
            out_specs=specs,
            scratch_shapes=stream_scratch(plan),
        ),
        input_output_aliases=aliases,
        compiler_params=params(20),
        cost_estimate=pl.CostEstimate(
            flops=6 * n_group * rows * feats, bytes_accessed=4 * feats * (rows + n_group), transcendentals=0
        ),
        name="back_group",
    )(where, values, high, low)
    return [tuple(result[2 * k : 2 * k + 2]) for k in range(len(plan.pairs[group]))], tuple(result[-2:])


class Pieces:
    def __init__(self, places, mine, theirs):
        self.places = (places, [tuple(p for place in places for p in place)])
        self.mine, self.theirs = mine, theirs

    def flat(self):
        return list(self.mine) + [self.theirs]


def gather_rows(plan, pair, chunks, s_ref, refs, position, target):
    core = s_ref[1]
    base = plan.pair_range(pair)[0]
    refs = list(refs)
    for c, places in zip(plan.pairs[pair], chunks):
        a, n = plan.chunks[c]
        h = n // 2
        for side, some in zip((core, 1 - core), places):
            for place in some:
                ref = refs.pop(0)
                if position in place:
                    k = place.index(position) * plan.block
                    target[pl.ds(pl.multiple_of(a - base + side * h, ROWS8), h), :] = ref[:, k : k + plan.block]


def forth_body(plan, pair, step, chunks, s_ref, *refs):
    nb = plan.nb
    refs = list(refs)
    scalar_ref = refs.pop(0) if step else None
    n_pieces = sum(len(some) for places in chunks for some in places)
    pieces, refs = refs[:n_pieces], refs[n_pieces:]
    direction_ref = refs.pop(0) if step else None
    high_hbm, low_hbm = refs[:2]
    n_ranges = len(tangent_ranges(plan, pair))
    target, acc, sums, high_buf, low_buf, sems = refs[-6:]
    vector_ref, outs = refs[-9 - 2 * n_ranges], refs[-8 - 2 * n_ranges : -8]
    n_pair = plan.pair_range(pair)[1]
    p = pl.program_id(0)
    high_ref, low_ref = stream(plan, p, (high_hbm, low_hbm), (high_buf, low_buf), sems)
    for position in range(nb):

        @pl.when(p == position)
        def _():
            gather_rows(plan, pair, chunks, s_ref, pieces, position, target)

    if step:
        direction = direction_ref[...]
        vector = direction - scalar_ref[0] * (target[...] + damping * direction)
    else:
        vector = -target[...]
    vector_ref[...] = vector
    part = dot3(vector, high_ref[...], low_ref[...], NT)
    square = jnp.sum(vector * vector).reshape(1, 1)
    cross = jnp.sum(vector * direction).reshape(1, 1) if step else square
    ids = lax.broadcasted_iota(jnp.int32, (ROWS8, plan.rows), 0)
    new = jnp.where(ids == 0, square, jnp.where(ids == 1, cross, 0.0))

    @pl.when(p == 0)
    def _():
        acc[:n_pair, :] = part
        sums[...] = new

    @pl.when(p > 0)
    def _():
        acc[:n_pair, :] += part
        sums[...] += new

    @pl.when(p == nb - 1)
    def _():
        acc[n_pair:, :] = sums[...]
        half = plan.rows // 2
        bit = s_ref[2]
        keep = pl.multiple_of(bit * half, LANES)
        send = pl.multiple_of((1 - bit) * half, LANES)
        for k, (a, n) in enumerate(tangent_ranges(plan, pair)):
            outs[2 * k][...] = acc[a : a + n, pl.ds(send, half)]
            outs[2 * k + 1][...] = acc[a : a + n, pl.ds(keep, half)]


def tangent_ranges(plan, pair):
    return [(0, plan.pair_range(pair)[1] + ROWS8)]


def placed(plan, pair):
    base, n_pair = plan.pair_range(pair)
    return pl.BlockSpec(
        (pl.Element(n_pair), pl.Element(plan.block)), lambda p, s: (base, (p ^ s[0]) * plan.block)
    )


def forth(plan, where, pair, pieces, high, low, vectors, step=None, direction=None):
    rows, block, feats, nb = plan.rows, plan.block, plan.feats, plan.nb
    half = rows // 2
    n_pair = plan.pair_range(pair)[1]
    operands, in_specs = [], []
    if step is not None:
        operands.append(step.reshape(1))
        in_specs.append(pl.BlockSpec(memory_space=pltpu.SMEM))
    for piece in pieces:
        for x in piece.flat():
            operands.append(x)
            in_specs.append(pl.BlockSpec(x.shape, lambda p, s: (0, 0), pipeline_mode=pl.Buffered(1)))
    if step is not None:
        operands.append(direction)
        in_specs.append(placed(plan, pair))
    n_ranges = len(tangent_ranges(plan, pair))
    aliases = {len(operands) + 1: 1 + 2 * n_ranges, len(operands) + 2: 2 + 2 * n_ranges}
    operands += [high, low]
    in_specs += [pl.BlockSpec(memory_space=pltpu.HBM)] * 2
    if vectors is not None:
        aliases[len(operands) + 1] = 0
        operands.append(vectors)
        in_specs.append(pl.BlockSpec(memory_space=pl.ANY))
    outs, specs = [pltpu.HBM((plan.classes, feats), F32)], [placed(plan, pair)]
    for _, n in tangent_ranges(plan, pair):
        outs += [jax.ShapeDtypeStruct((n, half), F32)] * 2
        specs += [pl.BlockSpec((n, half), lambda p, s: (0, 0))] * 2
    outs += [pltpu.HBM((rows, feats), BF16)] * 2
    specs += [pl.BlockSpec(memory_space=pltpu.HBM)] * 2
    result = pl.pallas_call(
        functools.partial(forth_body, plan, pair, step is not None, [piece.places for piece in pieces]),
        out_shape=outs,
        grid_spec=pltpu.PrefetchScalarGridSpec(
            num_scalar_prefetch=1,
            grid=(nb,),
            in_specs=in_specs,
            out_specs=specs,
            scratch_shapes=[
                pltpu.VMEM((n_pair, block), F32),
                pltpu.VMEM((n_pair + ROWS8, rows), F32),
                pltpu.VMEM((ROWS8, rows), F32),
            ]
            + stream_scratch(plan),
        ),
        input_output_aliases=aliases,
        compiler_params=params(46),
        cost_estimate=pl.CostEstimate(
            flops=6 * n_pair * rows * feats, bytes_accessed=4 * feats * (rows + 3 * n_pair), transcendentals=0
        ),
        name="forth_pair",
    )(where, *operands)
    return result[0], [tuple(result[1 + 2 * k : 3 + 2 * k]) for k in range(n_ranges)], tuple(result[-2:])


def last_body(plan, pair, chunks, s_ref, scalar_ref, *refs):
    nb = plan.nb
    refs = list(refs)
    n_pieces = sum(len(some) for places in chunks for some in places)
    pieces = refs[:n_pieces]
    direction_ref, residual_ref = refs[n_pieces : n_pieces + 2]
    out_ref, target, along, ready, arrived, left = refs[-6:]
    base, n_pair = plan.pair_range(pair)

    def place(ref, position):
        column = pl.multiple_of((position ^ s_ref[0]) * plan.block, LANES)
        return ref.at[pl.ds(base, n_pair), pl.ds(column, plan.block)]

    reads = []
    for q in range(nb):
        reads.append(pltpu.make_async_copy(place(direction_ref, q), along.at[q], arrived.at[0, q]))
        reads.append(pltpu.make_async_copy(place(residual_ref, q), ready.at[q], arrived.at[1, q]))
    writes = [pltpu.make_async_copy(ready.at[q], place(out_ref, q), left.at[q]) for q in range(nb)]
    for read in reads:
        read.start()
    for q in range(nb):
        gather_rows(plan, pair, chunks, s_ref, pieces, q, target)
        reads[2 * q].wait()
        reads[2 * q + 1].wait()
        residual = ready[q]
        following = residual + scalar_ref[1] * along[q]
        ready[q] = residual - scalar_ref[0] * (target[...] + damping * following)
        writes[q].start()
    for write in writes:
        write.wait()


def last(plan, where, pair, scalars, pieces, direction, residual, out):
    block, nb = plan.block, plan.nb
    n_pair = plan.pair_range(pair)[1]
    operands, in_specs = [where, scalars], [pl.BlockSpec(memory_space=pltpu.SMEM)] * 2
    for piece in pieces:
        for x in piece.flat():
            operands.append(x)
            in_specs.append(pl.BlockSpec(memory_space=pltpu.VMEM))
    operands += [direction, residual]
    aliases = {}
    if out is not None:
        aliases = {len(operands): 0}
        operands.append(out)
    in_specs += [pl.BlockSpec(memory_space=pl.ANY)] * (len(operands) - len(in_specs))
    return pl.pallas_call(
        functools.partial(last_body, plan, pair, [piece.places for piece in pieces]),
        out_shape=jax.ShapeDtypeStruct((plan.classes, plan.feats), F32),
        in_specs=in_specs,
        out_specs=pl.BlockSpec(memory_space=pl.ANY),
        scratch_shapes=[
            pltpu.VMEM((n_pair, block), F32),
            pltpu.VMEM((nb, n_pair, block), F32),
            pltpu.VMEM((nb, n_pair, block), F32),
            pltpu.SemaphoreType.DMA((2, nb)),
            pltpu.SemaphoreType.DMA((nb,)),
        ],
        input_output_aliases=aliases,
        compiler_params=params(22),
        cost_estimate=pl.CostEstimate(
            flops=6 * n_pair * plan.feats, bytes_accessed=16 * n_pair * plan.feats, transcendentals=0
        ),
        name="last_rows",
    )(*operands)


class Order:
    def __init__(self):
        self.token = None

    def after(self, x):
        if self.token is None:
            return x
        return lax.optimization_barrier((x, self.token))[0]

    def note(self, x):
        self.token = x


def columns(plan, x, positions):
    if list(positions) == list(range(positions[0], positions[-1] + 1)):
        return x[:, positions[0] * plan.block : (positions[-1] + 1) * plan.block]
    return jnp.concatenate([x[:, p * plan.block : (p + 1) * plan.block] for p in positions], axis=1)


class ClipSum:
    def __init__(self, plan, sides, turns):
        self.plan = plan
        self.own, other = sides
        levels = [(stride, 1 << k) for k, stride in enumerate(plan.levels)]
        down, up = (levels[::-1] if turn else levels for turn in turns)
        self.active = list(range(plan.nb))
        self.places, self.mine = [], []
        self.steps = [("core", 1, 0)]
        self.steps += [("scatter", stride, bit) for stride, bit in down]
        self.steps += [("double", stride, 0) for stride in plan.doubled]
        self.steps += [("gather", stride, bit) for stride, bit in up]
        self.kept = self.own
        self.pending = swap(other, "clip", 1)

    def done(self):
        return not self.steps

    def advance(self, order):
        kind, _, bit = self.steps.pop(0)
        got = order.after(self.pending)
        if kind == "gather":
            self.mine.append(got)
            self.places.append(tuple(p | bit for place in self.places for p in place))
        else:
            self.own = self.kept + got
            if not self.steps or self.steps[0][0] == "gather":
                self.places, self.mine = [tuple(self.active)], [self.own]
        kind, stride, bit = self.steps[0] if self.steps else ("core", 1, 0)
        if kind == "scatter":
            rest = [p for p in self.active if not p & bit]
            sent = columns(self.plan, self.own, [self.active.index(p | bit) for p in rest])
            self.kept = columns(self.plan, self.own, [self.active.index(p) for p in rest])
            self.active = rest
        elif kind == "double":
            sent = self.kept = self.own
        else:
            sent = self.mine[0] if len(self.mine) == 1 else jnp.concatenate(self.mine, axis=1)
        order.note(sent)
        self.pending = swap(sent, "clip", stride)

    def pieces(self, order):
        while not self.done():
            self.advance(order)
        return Pieces(self.places, self.mine, order.after(self.pending))


class FeatSum:
    def __init__(self, plan, halves, bit, axis):
        send, self.kept = halves
        self.bit, self.axis = bit, axis
        strides = [1 << k for k in range(plan.n_feat.bit_length() - 1)]
        self.strides = strides + [1]
        self.pending = swap(send, "feat", 1)

    def advance(self, order):
        self.strides.pop(0)
        got = order.after(self.pending)
        if self.strides:
            self.kept = self.kept + got
            self.pending = swap(self.kept, "feat", self.strides[0])
            order.note(self.kept)
        else:
            self.got = got
            order.note(got)

    def result(self, order):
        while self.strides:
            self.advance(order)
        one, two = [self.got, self.kept], [self.kept, self.got]
        return jnp.where(self.bit, jnp.concatenate(one, self.axis), jnp.concatenate(two, self.axis))


class ScalarSum:
    def __init__(self, plan, value):
        self.strides = [1 << k for k in range(plan.n_clip.bit_length() - 1)]
        self.row = jnp.broadcast_to(value, (ROWS8, LANES))
        self.pending = swap(self.row, "clip", 1)

    def advance(self, order):
        if not self.strides:
            return
        self.strides.pop(0)
        self.row = self.row + order.after(self.pending)
        order.note(self.row)
        if self.strides:
            self.pending = swap(self.row, "clip", self.strides[0])

    def result(self, order):
        while self.strides:
            self.advance(order)
        return self.row[0, 0]


def local(features, weights, labels):
    rows, feats = features.shape
    classes = weights.shape[0]
    plan = Plan(rows, feats, classes, lax.axis_size("clip"), lax.axis_size("feat"))
    total_rows = rows * plan.n_clip
    me, bit = lax.axis_index("clip"), lax.axis_index("feat") & 1
    mask = sum(((me // stride) & 1) << k for k, stride in enumerate(plan.levels))
    where = jnp.stack([jnp.asarray(mask), me & 1, bit]).astype(jnp.int32)
    order = Order()
    groups = range(len(plan.pairs))

    split, parts = None, []
    for part in range(rows // plan.rows_step):
        if part > 1:
            parts[part - 2].advance(order)
        split, halves = first(plan, where, order.after(features), weights, part, split)
        order.note(halves[0])
        parts.append(FeatSum(plan, halves, bit, 0))
    for summed in parts:
        summed.advance(order)
    split = list(split)
    probs, values = [], []
    for part, summed in enumerate(parts):
        logits = summed.result(order)
        top = jnp.max(logits, axis=0, keepdims=True)
        powers = jnp.exp(logits - top)
        some = powers / jnp.sum(powers, axis=0, keepdims=True)
        mine = labels[part * plan.rows_step : (part + 1) * plan.rows_step]
        onehot = (mine[None, :] == jnp.arange(classes, dtype=jnp.int32)[:, None]).astype(F32)
        probs.append(some)
        values.append((some - onehot) / total_rows)
    probs, values = jnp.concatenate(probs, axis=1), jnp.concatenate(values, axis=1)

    def backward(values, scalar=None, during=None, under=None):
        sums, result = [None] * len(plan.chunks), None

        def multiply(group):
            a, n = plan.pair_range(group)
            sides, split[:] = back(plan, where, group, order.after(values[a : a + n]), *split)
            for c, side in zip(plan.pairs[group], sides):
                sums[c] = ClipSum(plan, side, plan.turns[c])
            order.note(sides[-1][0])

        def go(*chunks):
            for c in chunks:
                if not sums[c].done():
                    sums[c].advance(order)

        multiply(0)
        if scalar is not None:
            scalar.advance(order)
        go(0, 1)
        multiply(1)
        if scalar is not None:
            scalar.advance(order)
        go(0, 1, 2, 3)
        if scalar is not None:
            result = during(scalar.result(order))
        if under is not None:
            result = under(result)
        go(0, 1, 2, 3, 0, 1, 2, 3, 2, 3, 0, 1)
        return sums, go, result

    def forward(sums, go, step=None, direction=None):
        vectors, found = None, []

        def multiply(group):
            pieces = [sums[c].pieces(order) for c in plan.pairs[group]]
            out, halves, split[:] = forth(plan, where, group, pieces, *split, vectors, step, direction)
            order.note(halves[0][0])
            found.append(FeatSum(plan, halves[0], bit, 1))
            return out

        vectors = multiply(0)
        go(2, 3)
        found[0].advance(order)
        vectors = multiply(1)
        for k in (0, 1, 0, 1):
            if found[k].strides:
                found[k].advance(order)
        tangents = [f.result(order) for f in found]
        inner = sum(t[-ROWS8 : 2 - ROWS8, 0] for t in tangents)
        return vectors, jnp.concatenate([t[:-ROWS8] for t in tangents], axis=0), inner

    def bend(tangent):
        weighted = probs * tangent
        bent = (weighted - probs * jnp.sum(weighted, axis=0, keepdims=True)) / total_rows
        order.note(bent)
        return bent, ScalarSum(plan, jnp.sum(bent * tangent))

    sums, go, _ = backward(values)
    direction, tangent, inner = forward(sums, go)
    norm0 = inner[0]
    bent, curvature = bend(tangent)

    sums, go, step0 = backward(bent, curvature, lambda total: norm0 / (total + damping * norm0))
    residual, fresh, inner = forward(sums, go, step0, direction)
    norm1, cross = inner[0], inner[1]
    ratio = norm1 / norm0
    bent, curvature = bend(fresh + ratio * tangent)
    length = norm1 + 2.0 * ratio * cross + ratio * ratio * norm0

    def under(step1):
        moved = order.after(weights) + (step0 + step1 * ratio) * direction + step1 * residual
        order.note(moved)
        return step1, moved

    sums, go, (step1, moved) = backward(
        bent, curvature, lambda total: norm1 / (total + damping * length), under
    )
    scalars, out = jnp.stack([step1, ratio]), None
    for group, members in enumerate(plan.pairs):
        pieces = [sums[c].pieces(order) for c in members]
        if group == 0:
            go(2, 3)
        out = last(plan, where, group, scalars, pieces, direction, residual, out)
        order.note(out)
    return moved, out


def solution(mesh):
    in_specs = (P("clip", "feat"), P(None, "feat"), P("clip"))
    out_specs = (P(None, "feat"), P(None, "feat"))
    return jax.shard_map(local, mesh=mesh, in_specs=in_specs, out_specs=out_specs, check_vma=False)
```
